32 devices in a mesh: grid: 16 (over z, x, core), orb: 2 (over y).
Axes of the slice: x: 2, y: 2, z: 4, core: 2. Of those that a mesh axis runs over, the one named last changes fastest.
Arguments:
- wave: float32 [2, 2, 128, 128, 128], P(None, 'orb', 'grid'), may hold values from -6 to 6
- potential: float32 [128, 128, 128], P('grid'), may hold values from -24 to 24
- occupations: float32 [2], P('orb'), may hold values from 0.01 to 0.1
- centres: int32 [3, 128], replicated, may hold values from 0 to 127, as said below
- species: int32 [128], replicated, may hold values from 0 to 1
- projectors: float32 [2, 16, 8, 256], replicated, may hold values from -0.75 to 0.75
- coupling: float32 [2, 8, 8], replicated, may hold values from -6 to 6
Outputs:
- update: float32 [2, 2, 128, 128, 128], P(None, 'orb', 'grid')
- density: float32 [128, 128, 128], P('grid', 'orb')
The draws below stay inside these ranges and needn't reach their ends.
Inputs may be any that keep to these rules, and one draw needn't show every extreme that they name: `centres`: each column is a grid point of the cell.
All inputs are finite; a program needn't handle non-finite values.
Results may differ from the reference program's by a relative error of at most 0.0003.
Values sent between devices are 32-bit elements; how exact they have to be, the bound alone decides.
A program may use at most 64 MiB of HBM per device.

```python
import math
import jax
import jax.numpy as jnp
from jax import lax

SIDE = 128
NPROJ = 8
SPECIES = 2
BOX = 16
ATOMS = 128
ORBS = 2


def draw_centres(key, part):
    place_key = jax.random.fold_in(key, 11)
    pick_key = jax.random.fold_in(key, 12)
    coords = jax.random.randint(place_key, (3, ATOMS), 0, SIDE, dtype=jnp.int32)
    chosen = jax.random.randint(pick_key, (), 0, ATOMS, dtype=jnp.int32)
    second_atom = (chosen + 1) % ATOMS
    coords = coords.at[:, chosen].set(SIDE - 1)
    coords = coords.at[:, second_atom].set(0)
    return coords


def touch_ends(values, rng, smallest, top_value):
    spot = [jax.random.randint(jax.random.fold_in(rng, axis), (), 0, length) for axis, length in enumerate(values.shape)]
    longest = values.shape.index(max(values.shape))
    beside = spot[:longest] + [(spot[longest] + 1) % values.shape[longest]] + spot[longest + 1:]
    return values.at[tuple(spot)].set(smallest).at[tuple(beside)].set(top_value)


def levels(key, shape, split, smallest, largest):
    def one(position, parts):
        steps = jax.random.uniform(jax.random.fold_in(jax.random.fold_in(key, 6), position), (parts,), jnp.float32, smallest / len(split), largest / len(split))
        return jnp.repeat(jnp.exp(steps), shape[position] // parts).reshape((-1,) + (1,) * (len(shape) - position - 1))

    factor_of = one(*split[0])
    for cut in split[1:]:
        factor_of = factor_of * one(*cut)
    return factor_of


def noise(key, shape, deviation, bound, cuts=(), kind=jnp.bfloat16):
    entries = jax.random.normal(key, shape, jnp.float32) * deviation
    if len(cuts) > 0:
        entries = levels(key, shape, cuts, -0.22, 0.18) * entries
    return jnp.clip(entries, min=-bound, max=bound).astype(kind)


def setup_inputs(seed: int = 0) -> dict:
    key_of = jax.random.split(jax.random.key(seed), 8)
    return {
        "wave": noise(key_of[0], (2, ORBS, SIDE, SIDE, SIDE), 1.0, 6.0, ((1, 2), (2, 16)), jnp.float32),
        "potential": noise(key_of[1], (SIDE, SIDE, SIDE), 4.0, 24.0, ((0, 16),), jnp.float32),
        "occupations": jnp.clip(jnp.exp(math.log(0.1) - 2.3025851 * jax.random.uniform(key_of[2], (ORBS,), jnp.float32) ** levels(key_of[2], (ORBS,), ((0, 2),), -0.2, 0.2)), 0.01, 0.1),
        "centres": draw_centres(jax.random.fold_in(key_of[7], 71), 0),
        "species": touch_ends(jax.random.randint(key_of[4], (ATOMS,), 0, SPECIES), jax.random.fold_in(key_of[4], 1), 0, SPECIES - 1).astype(jnp.int32),
        "projectors": noise(key_of[5], (SPECIES, BOX, NPROJ, BOX * BOX), 0.125, 0.75, (), jnp.float32),
        "coupling": noise(key_of[6], (SPECIES, NPROJ, NPROJ), 1.0, 6.0, (), jnp.float32),
    }


spacing = 0.32
time_step = 0.1
highest = lax.Precision.HIGHEST


def frequencies(extent):
    counts = jnp.arange(extent, dtype=jnp.int32)
    signed = jnp.where(counts < extent // 2, counts, counts - extent)
    return signed.astype(jnp.float32) * (2.0 * math.pi / (extent * spacing))


def reference(wave, potential, occupations, centres, species, projectors, coupling):
    waves_k = frequencies(SIDE)
    kinetic = 0.5 * (waves_k[:, None, None] ** 2 + waves_k[None, :, None] ** 2 + waves_k[None, None, :] ** 2)

    def local_terms(halves):
        real_part, imag_part = halves
        spectrum = jnp.fft.fftn(lax.complex(real_part, imag_part))
        returned = jnp.fft.ifftn(spectrum * kinetic)
        return (jnp.real(returned) + potential * real_part, jnp.imag(returned) + potential * imag_part)

    h_real, h_imag = lax.map(local_terms, (wave[0], wave[1]))
    offsets = jnp.arange(BOX, dtype=jnp.int32) - BOX // 2
    flat_real = wave[0].reshape(ORBS, -1)
    flat_imag = wave[1].reshape(ORBS, -1)

    def add_atom(totals, atom_data):
        acc_real, acc_imag = totals
        centre, species_id = atom_data
        rows_x = (centre[0] + offsets) % SIDE
        rows_y = (centre[1] + offsets) % SIDE
        rows_z = (centre[2] + offsets) % SIDE
        grid_points = ((rows_x[:, None, None] * SIDE + rows_y[None, :, None]) * SIDE + rows_z[None, None, :]).reshape(-1).astype(jnp.int32)
        projector_rows = jnp.transpose(projectors[species_id], (1, 0, 2)).reshape(NPROJ, -1)
        coef_real = jnp.dot(projector_rows, flat_real[:, grid_points].T, precision=highest)
        coef_imag = jnp.dot(projector_rows, flat_imag[:, grid_points].T, precision=highest)
        scaled_real = jnp.dot(coupling[species_id], coef_real, precision=highest)
        scaled_imag = jnp.dot(coupling[species_id], coef_imag, precision=highest)
        acc_real = acc_real.at[:, grid_points].add(jnp.dot(scaled_real.T, projector_rows, precision=highest))
        acc_imag = acc_imag.at[:, grid_points].add(jnp.dot(scaled_imag.T, projector_rows, precision=highest))
        return (acc_real, acc_imag), None

    start_totals = (jnp.zeros(flat_real.shape, jnp.float32), jnp.zeros(flat_imag.shape, jnp.float32))
    (nl_real, nl_imag), _ = lax.scan(add_atom, start_totals, (centres.T, species))
    total_real = h_real + nl_real.reshape(h_real.shape)
    total_imag = h_imag + nl_imag.reshape(h_imag.shape)
    half_step = 0.5 * time_step
    update = jnp.stack([half_step * total_imag, -half_step * total_real])
    density = jnp.tensordot(occupations, wave[0] * wave[0] + wave[1] * wave[1], axes=1, precision=highest)
    return update, density
```

```python
import math

import jax
import jax.numpy as jnp
import numpy as np
from jax import lax
from jax.experimental import pallas as pl
from jax.experimental.pallas import tpu as pltpu
from jax.sharding import PartitionSpec as P

spacing = 0.32
time_step = 0.1
highest = lax.Precision.HIGHEST
VMEM = pl.BlockSpec(memory_space=pltpu.VMEM)
SMEM = pl.BlockSpec(memory_space=pltpu.SMEM)


def params():
    return pltpu.CompilerParams(vmem_limit_bytes=40 * 1024 * 1024)


def second_derivative(extent):
    counts = np.arange(extent)
    signed = np.where(counts < extent // 2, counts, counts - extent)
    waves = signed * (2.0 * math.pi / (extent * spacing))
    angles = (counts[:, None] * counts[None, :] % extent) * (2.0 * math.pi / extent)
    row = np.cos(angles) @ (0.5 * waves**2) / extent
    full = row[(counts[:, None] - counts[None, :]) % extent].astype(np.float32)
    high = full.astype(jnp.bfloat16)
    low = (full - high.astype(np.float32)).astype(jnp.bfloat16)
    return jnp.asarray(high), jnp.asarray(low)


def split(value):
    high = value.astype(jnp.bfloat16)
    low = (value - high.astype(jnp.float32)).astype(jnp.bfloat16)
    return high, low


def mul(left, right):
    def dot(a, b):
        return jnp.dot(a, b, preferred_element_type=jnp.float32)

    return dot(left[0], right[0]) + (dot(left[0], right[1]) + dot(left[1], right[0]))


def pack_kernel(wave_ref, occ_ref, send_ref, density_ref):
    _, orbitals, planes, extent, _ = wave_ref.shape
    count = send_ref.shape[0]
    width = extent // count
    for p in range(planes):
        total = None
        for o in range(orbitals):
            real = wave_ref[0, o, p]
            imag = wave_ref[1, o, p]
            term = occ_ref[o] * (real * real + imag * imag)
            total = term if total is None else total + term
        density_ref[p] = total
        for c in range(2):
            for o in range(orbitals):
                for d in range(count):
                    send_ref[d, c * orbitals + o, pl.ds(p, width, stride=planes), :] = wave_ref[
                        c, o, p, d * width : (d + 1) * width, :
                    ]


def along_x_kernel(held_ref, high_ref, low_ref, out_ref, lined):
    count, rows, both, extent = held_ref.shape
    planes = extent // count
    matrix = (high_ref[...], low_ref[...])
    for r in range(rows):
        for y in range(both // planes):
            block = pl.ds(y * planes, planes)
            if planes % 8 == 0:
                column = held_ref[:, r, block, :].reshape(extent, extent)
            else:
                for s in range(count):
                    lined[s * planes : (s + 1) * planes, :] = held_ref[s, r, block, :]
                column = lined[...]
            result = mul(matrix, split(column))
            if planes % 8 == 0:
                out_ref[:, r, block, :] = result.reshape(count, planes, extent)
            else:
                lined[...] = result
                for s in range(count):
                    out_ref[s, r, block, :] = lined[s * planes : (s + 1) * planes, :]


def list_hits(centres_ref, hits, extent, planes, half_box):
    first_plane = lax.axis_index("grid") * planes

    def look(atom, found):
        start = lax.rem(first_plane - centres_ref[0, atom] + (half_box + extent), extent)
        hits[found] = atom
        meets = jnp.logical_or(start < 2 * half_box, start + planes > extent)
        return found + meets.astype(jnp.int32)

    return lax.fori_loop(0, centres_ref.shape[1], look, jnp.int32(0), unroll=8)


def atom_place(centres_ref, species_ref, atom, extent, planes, box):
    half_box = box // 2
    first_plane = lax.axis_index("grid") * planes
    start_x = lax.rem(first_plane - centres_ref[0, atom] + (half_box + extent), extent)
    start_y = lax.rem(centres_ref[1, atom] + (extent - half_box), extent)
    start_z = lax.rem(centres_ref[2, atom] + (extent - half_box), extent)
    slots = []
    for p in range(planes):
        depth = lax.rem(start_x + p, extent)
        slots.append(species_ref[atom] * (box + 1) + jnp.minimum(depth, box))
    return slots, start_y, start_z


def project_kernel(wave_ref, table_ref, centres_ref, species_ref, coef_ref, padded, sums, hits):
    _, orbitals, planes, extent, _ = wave_ref.shape
    box = table_ref.shape[1]
    lanes = table_ref.shape[2]
    rows = 2 * orbitals
    for c in range(2):
        for o in range(orbitals):
            for p in range(planes):
                at = (c * orbitals + o) * planes + p
                padded[at, :extent, :] = wave_ref[c, o, p]
                padded[at, extent:, :] = wave_ref[c, o, p, :box, :]
    sums[...] = jnp.zeros_like(sums)
    found = list_hits(centres_ref, hits, extent, planes, box // 2)
    lane = lax.broadcasted_iota(jnp.int32, (box, lanes), 1) % box

    def one(step, carry):
        atom = hits[step]
        slots, start_y, start_z = atom_place(
            centres_ref, species_ref, atom, extent, planes, box
        )
        places = lane + start_z
        places = jnp.where(places >= extent, places - extent, places)
        totals = [None] * rows
        for p in range(planes):
            beta = table_ref[slots[p]]
            for r in range(rows):
                window = padded[r * planes + p, pl.ds(start_y, box), :]
                spread_out = jnp.take_along_axis(window, places, axis=1, mode="promise_in_bounds")
                term = spread_out * beta
                totals[r] = term if totals[r] is None else totals[r] + term
        for r in range(rows):
            sums[r, pl.ds(atom, 1), :] = jnp.sum(totals[r], axis=0, keepdims=True)
        return carry

    lax.fori_loop(0, found, one, 0)
    proj_count = lanes // box
    group = lax.broadcasted_iota(jnp.int32, (proj_count, lanes), 1) // box
    member = (group == lax.broadcasted_iota(jnp.int32, (proj_count, lanes), 0)).astype(jnp.float32)
    for r in range(rows):
        coef_ref[r] = lax.dot_general(
            member,
            sums[r],
            (((1,), (1,)), ((), ())),
            precision=highest,
            preferred_element_type=jnp.float32,
        )


def spread_kernel(
    wave_ref,
    potential_ref,
    table_ref,
    coef_ref,
    coupling_ref,
    kinds_ref,
    centres_ref,
    species_ref,
    high_ref,
    low_ref,
    out_ref,
    factors,
    hits,
):
    _, orbitals, planes, extent, _ = wave_ref.shape
    box = table_ref.shape[1]
    lanes = table_ref.shape[2]
    proj_count = lanes // box
    rows = 2 * orbitals
    group = lax.broadcasted_iota(jnp.int32, (proj_count, lanes), 1) // box
    member = (group == lax.broadcasted_iota(jnp.int32, (proj_count, lanes), 0)).astype(jnp.float32)
    kinds = kinds_ref[...]
    for r in range(rows):
        scaled = None
        for s in range(coupling_ref.shape[0]):
            term = jnp.dot(
                coupling_ref[s],
                coef_ref[r],
                precision=highest,
                preferred_element_type=jnp.float32,
            )
            term = jnp.where(kinds == s, term, 0.0)
            scaled = term if scaled is None else scaled + term
        factors[r] = lax.dot_general(
            scaled,
            member,
            (((0,), (0,)), ((), ())),
            precision=highest,
            preferred_element_type=jnp.float32,
        )
    matrix = (high_ref[...], low_ref[...])
    for c in range(2):
        for o in range(orbitals):
            for p in range(planes):
                at = (c * orbitals + o) * planes + p
                value = wave_ref[c, o, p]
                parts = split(value)
                out_ref[at, :extent, :] = (
                    mul(matrix, parts) + mul(parts, matrix) + potential_ref[p] * value
                )
                out_ref[at, extent:, :] = jnp.zeros((box, extent), jnp.float32)
    found = list_hits(centres_ref, hits, extent, planes, box // 2)
    lane = lax.broadcasted_iota(jnp.int32, (box, extent), 1)

    def one(step, carry):
        atom = hits[step]
        slots, start_y, start_z = atom_place(
            centres_ref, species_ref, atom, extent, planes, box
        )
        away = lane - start_z
        inside = jnp.where(away < 0, away + extent, away) < box
        turn = lax.rem(start_z, box)
        factor = [factors[r, pl.ds(atom, 1), :] for r in range(rows)]
        for p in range(planes):
            beta = table_ref[slots[p]]
            for r in range(rows):
                term = beta * factor[r]
                reach = lanes // 2
                while reach >= box:
                    term = term + pltpu.roll(term, reach, 1)
                    reach //= 2
                term = jnp.where(inside, pltpu.roll(term, turn, 1), 0.0)
                out_ref[r * planes + p, pl.ds(start_y, box), :] += term
        return carry

    lax.fori_loop(0, found, one, 0)


def finish_kernel(local_ref, along_ref, out_ref):
    _, orbitals, planes, extent, _ = out_ref.shape
    count = along_ref.shape[0]
    width = extent // count
    box = local_ref.shape[1] - extent
    half_step = 0.5 * time_step
    for c in range(2):
        factor = half_step if c == 1 else -half_step
        for o in range(orbitals):
            r = c * orbitals + o
            for p in range(planes):
                for d in range(count):
                    total = (
                        local_ref[r * planes + p, d * width : (d + 1) * width, :]
                        + along_ref[d, r, pl.ds(p, width, stride=planes), :]
                    )
                    if d * width < box:
                        total += local_ref[
                            r * planes + p, extent + d * width : extent + (d + 1) * width, :
                        ]
                    out_ref[1 - c, o, p, d * width : (d + 1) * width, :] = factor * total


def shape(dims):
    return jax.ShapeDtypeStruct(dims, jnp.float32)


def cost(flops, size):
    return pl.CostEstimate(flops=flops, bytes_accessed=size, transcendentals=0)


def per_device(wave, potential, occupations, centres, species, projectors, coupling):
    _, orbitals, planes, extent, _ = wave.shape
    kind_count, box, proj_count, _ = projectors.shape
    atom_count = species.shape[0]
    count = lax.axis_size("grid")
    rows = 2 * orbitals
    width = extent // count
    lanes = proj_count * box
    size = wave.size * 4
    high, low = second_derivative(extent)
    send, density_term = pl.pallas_call(
        pack_kernel,
        out_shape=(shape((count, rows, width * planes, extent)), shape((planes, extent, extent))),
        in_specs=[VMEM, SMEM],
        out_specs=(VMEM, VMEM),
        compiler_params=params(),
        cost_estimate=cost(wave.size, 2 * size),
        name="pack",
    )(wave, occupations)
    held = lax.all_to_all(send, "grid", 0, 0, tiled=True)
    density = lax.psum_scatter(density_term, "orb", scatter_dimension=1, tiled=True)
    table = projectors.reshape(kind_count, box, proj_count, box, box)
    table = jnp.transpose(table, (0, 1, 3, 2, 4)).reshape(kind_count, box, box, lanes)
    table = jnp.pad(table, ((0, 0), (0, 1), (0, 0), (0, 0)))
    table = table.reshape(kind_count * (box + 1), box, lanes)
    coef = pl.pallas_call(
        project_kernel,
        out_shape=shape((rows, proj_count, atom_count)),
        in_specs=[VMEM, VMEM, SMEM, SMEM],
        out_specs=VMEM,
        scratch_shapes=[
            pltpu.VMEM((rows * planes, extent + box, extent), jnp.float32),
            pltpu.VMEM((rows, atom_count, lanes), jnp.float32),
            pltpu.SMEM((atom_count + 8,), jnp.int32),
        ],
        compiler_params=params(),
        cost_estimate=cost(40 * wave.size, 20 * size),
        name="project",
    )(wave, table, centres, species)
    coef = lax.psum(coef, "grid")
    along = pl.pallas_call(
        along_x_kernel,
        out_shape=shape(held.shape),
        in_specs=[VMEM, VMEM, VMEM],
        out_specs=VMEM,
        scratch_shapes=[pltpu.VMEM((extent, extent), jnp.float32)],
        compiler_params=params(),
        cost_estimate=cost(6 * extent * wave.size, 2 * size),
        name="along_x",
    )(held, high, low)
    back = lax.all_to_all(along, "grid", 0, 0, tiled=True)
    local = pl.pallas_call(
        spread_kernel,
        out_shape=shape((rows * planes, extent + box, extent)),
        in_specs=[VMEM] * 6 + [SMEM, SMEM] + [VMEM] * 2,
        out_specs=VMEM,
        scratch_shapes=[
            pltpu.VMEM((rows, atom_count, lanes), jnp.float32),
            pltpu.SMEM((atom_count + 8,), jnp.int32),
        ],
        compiler_params=params(),
        cost_estimate=cost(40 * wave.size, 20 * size),
        name="spread",
    )(
        wave,
        potential,
        table,
        coef,
        coupling,
        species.reshape(1, atom_count),
        centres,
        species,
        high,
        low,
    )
    update = pl.pallas_call(
        finish_kernel,
        out_shape=shape(wave.shape),
        in_specs=[VMEM, VMEM],
        out_specs=VMEM,
        compiler_params=params(),
        cost_estimate=cost(4 * wave.size, 3 * size),
        name="finish",
    )(local, back)
    return (update, density)


def solution(mesh):
    placed = (
        P(None, "orb", "grid", None, None),
        P("grid", None, None),
        P("orb"),
        P(),
        P(),
        P(),
        P(),
    )
    return jax.shard_map(
        per_device,
        mesh=mesh,
        in_specs=placed,
        out_specs=(P(None, "orb", "grid", None, None), P("grid", "orb", None)),
        check_vma=False,
    )
```

```python
import math

import jax
import jax.numpy as jnp
import numpy as np
from jax import lax
from jax.experimental import pallas as pl
from jax.experimental.pallas import tpu as pltpu
from jax.sharding import PartitionSpec as P

spacing = 0.32
time_step = 0.1
highest = lax.Precision.HIGHEST
VMEM = pl.BlockSpec(memory_space=pltpu.VMEM)
SMEM = pl.BlockSpec(memory_space=pltpu.SMEM)


def passed_along(value, steps):
    count = lax.axis_size("grid")
    pairs = [(source, (source + steps) % count) for source in range(count)]
    return lax.ppermute(value, "grid", pairs)


def params():
    return pltpu.CompilerParams(vmem_limit_bytes=40 * 1024 * 1024)


def second_derivative(extent):
    counts = np.arange(extent)
    signed = np.where(counts < extent // 2, counts, counts - extent)
    waves = signed * (2.0 * math.pi / (extent * spacing))
    angles = (counts[:, None] * counts[None, :] % extent) * (2.0 * math.pi / extent)
    row = np.cos(angles) @ (0.5 * waves**2) / extent
    full = row[(counts[:, None] - counts[None, :]) % extent].astype(np.float32)
    high = full.astype(jnp.bfloat16)
    low = (full - high.astype(np.float32)).astype(jnp.bfloat16)
    return jnp.asarray(np.stack([high, low]))


def split(value):
    high = value.astype(jnp.bfloat16)
    low = (value - high.astype(jnp.float32)).astype(jnp.bfloat16)
    return high, low


def mul(left, right):
    def dot(a, b):
        return jnp.dot(a, b, preferred_element_type=jnp.float32)

    return dot(left[0], right[0]) + (dot(left[0], right[1]) + dot(left[1], right[0]))


def pack_kernel(wave_ref, occ_ref, send_ref, density_ref):
    _, orbitals, planes, extent, _ = wave_ref.shape
    count = send_ref.shape[0]
    width = extent // count
    for p in range(planes):
        total = None
        for o in range(orbitals):
            real = wave_ref[0, o, p]
            imag = wave_ref[1, o, p]
            term = occ_ref[o] * (real * real + imag * imag)
            total = term if total is None else total + term
        density_ref[p] = total
        for c in range(2):
            for o in range(orbitals):
                for d in range(count):
                    send_ref[d, c * orbitals + o, pl.ds(p, width, stride=planes), :] = wave_ref[
                        c, o, p, d * width : (d + 1) * width, :
                    ]


def along_x_kernel(held_ref, matrix_ref, coef_ref, out_ref, lined):
    count, rows, both, extent = held_ref.shape
    planes = extent // count
    matrix = (matrix_ref[0], matrix_ref[1])
    for r in range(rows):
        for y in range(both // planes):
            block = pl.ds(y * planes, planes)
            if planes % 8 == 0:
                column = held_ref[:, r, block, :].reshape(extent, extent)
            else:
                for s in range(count):
                    lined[s * planes : (s + 1) * planes, :] = held_ref[s, r, block, :]
                column = lined[...]
            result = mul(matrix, split(column))
            if planes % 8 == 0:
                out_ref[:, r, block, :] = result.reshape(count, planes, extent)
            else:
                lined[...] = result
                for s in range(count):
                    out_ref[s, r, block, :] = lined[s * planes : (s + 1) * planes, :]


def list_hits(centres_ref, hits, extent, planes, half_box):
    first_plane = lax.axis_index("grid") * planes

    def look(atom, found):
        start = lax.rem(first_plane - centres_ref[0, atom] + (half_box + extent), extent)
        hits[found] = atom
        meets = jnp.logical_or(start < 2 * half_box, start + planes > extent)
        return found + meets.astype(jnp.int32)

    return lax.fori_loop(0, centres_ref.shape[1], look, jnp.int32(0), unroll=8)


def atom_place(centres_ref, species_ref, atom, extent, planes, box):
    half_box = box // 2
    first_plane = lax.axis_index("grid") * planes
    start_x = lax.rem(first_plane - centres_ref[0, atom] + (half_box + extent), extent)
    start_y = lax.rem(centres_ref[1, atom] + (extent - half_box), extent)
    start_z = lax.rem(centres_ref[2, atom] + (extent - half_box), extent)
    slots = []
    for p in range(planes):
        depth = lax.rem(start_x + p, extent)
        slots.append(species_ref[atom] * (box + 1) + jnp.minimum(depth, box))
    return slots, start_y, start_z


def project_kernel(
    wave_ref,
    table_ref,
    coupling_ref,
    kinds_ref,
    centres_ref,
    species_ref,
    coef_ref,
    padded,
    sums,
    hits,
):
    _, orbitals, planes, extent, _ = wave_ref.shape
    box = table_ref.shape[1]
    lanes = table_ref.shape[2]
    rows = 2 * orbitals
    for c in range(2):
        for o in range(orbitals):
            for p in range(planes):
                at = (c * orbitals + o) * planes + p
                padded[at, :extent, :] = wave_ref[c, o, p]
                padded[at, extent:, :] = wave_ref[c, o, p, :box, :]
    sums[...] = jnp.zeros_like(sums)
    found = list_hits(centres_ref, hits, extent, planes, box // 2)
    lane = lax.broadcasted_iota(jnp.int32, (box, lanes), 1) % box

    def one(step, carry):
        atom = hits[step]
        slots, start_y, start_z = atom_place(
            centres_ref, species_ref, atom, extent, planes, box
        )
        places = lane + start_z
        places = jnp.where(places >= extent, places - extent, places)
        totals = [None] * rows
        for p in range(planes):
            beta = table_ref[slots[p]]
            for r in range(rows):
                window = padded[r * planes + p, pl.ds(start_y, box), :]
                spread_out = jnp.take_along_axis(window, places, axis=1, mode="promise_in_bounds")
                term = spread_out * beta
                totals[r] = term if totals[r] is None else totals[r] + term
        for r in range(rows):
            sums[r, pl.ds(atom, 1), :] = jnp.sum(totals[r], axis=0, keepdims=True)
        return carry

    lax.fori_loop(0, found, one, 0)
    proj_count = lanes // box
    group = lax.broadcasted_iota(jnp.int32, (proj_count, lanes), 1) // box
    member = (group == lax.broadcasted_iota(jnp.int32, (proj_count, lanes), 0)).astype(jnp.float32)
    kinds = kinds_ref[...]
    for r in range(rows):
        partial = lax.dot_general(
            member,
            sums[r],
            (((1,), (1,)), ((), ())),
            precision=highest,
            preferred_element_type=jnp.float32,
        )
        scaled = None
        for s in range(coupling_ref.shape[0]):
            term = jnp.dot(
                coupling_ref[s], partial, precision=highest, preferred_element_type=jnp.float32
            )
            term = jnp.where(kinds == s, term, 0.0)
            scaled = term if scaled is None else scaled + term
        coef_ref[r] = scaled


def local_kernel(wave_ref, potential_ref, matrix_ref, out_ref):
    _, orbitals, planes, extent, _ = wave_ref.shape
    box = out_ref.shape[1] - extent
    matrix = (matrix_ref[0], matrix_ref[1])
    for c in range(2):
        for o in range(orbitals):
            for p in range(planes):
                at = (c * orbitals + o) * planes + p
                value = wave_ref[c, o, p]
                parts = split(value)
                out_ref[at, :extent, :] = (
                    mul(matrix, parts) + mul(parts, matrix) + potential_ref[p] * value
                )
                out_ref[at, extent:, :] = jnp.zeros((box, extent), jnp.float32)


def spread_kernel(local_ref, table_ref, coef_ref, centres_ref, species_ref, out_ref, factors, hits):
    box = table_ref.shape[1]
    lanes = table_ref.shape[2]
    extent = local_ref.shape[2]
    rows = coef_ref.shape[0]
    planes = local_ref.shape[0] // rows
    proj_count = lanes // box
    group = lax.broadcasted_iota(jnp.int32, (proj_count, lanes), 1) // box
    member = (group == lax.broadcasted_iota(jnp.int32, (proj_count, lanes), 0)).astype(jnp.float32)
    for r in range(rows):
        factors[r] = lax.dot_general(
            coef_ref[r],
            member,
            (((0,), (0,)), ((), ())),
            precision=highest,
            preferred_element_type=jnp.float32,
        )
    out_ref[...] = local_ref[...]
    found = list_hits(centres_ref, hits, extent, planes, box // 2)
    lane = lax.broadcasted_iota(jnp.int32, (box, extent), 1)

    def one(step, carry):
        atom = hits[step]
        slots, start_y, start_z = atom_place(
            centres_ref, species_ref, atom, extent, planes, box
        )
        away = lane - start_z
        inside = jnp.where(away < 0, away + extent, away) < box
        turn = lax.rem(start_z, box)
        factor = [factors[r, pl.ds(atom, 1), :] for r in range(rows)]
        for p in range(planes):
            beta = table_ref[slots[p]]
            for r in range(rows):
                term = beta * factor[r]
                reach = lanes // 2
                while reach >= box:
                    term = term + pltpu.roll(term, reach, 1)
                    reach //= 2
                term = jnp.where(inside, pltpu.roll(term, turn, 1), 0.0)
                out_ref[r * planes + p, pl.ds(start_y, box), :] += term
        return carry

    lax.fori_loop(0, found, one, 0)


def finish_kernel(local_ref, along_ref, out_ref):
    _, orbitals, planes, extent, _ = out_ref.shape
    count = along_ref.shape[0]
    width = extent // count
    box = local_ref.shape[1] - extent
    half_step = 0.5 * time_step
    for c in range(2):
        factor = half_step if c == 1 else -half_step
        for o in range(orbitals):
            r = c * orbitals + o
            for p in range(planes):
                for d in range(count):
                    total = (
                        local_ref[r * planes + p, d * width : (d + 1) * width, :]
                        + along_ref[d, r, pl.ds(p, width, stride=planes), :]
                    )
                    if d * width < box:
                        total += local_ref[
                            r * planes + p, extent + d * width : extent + (d + 1) * width, :
                        ]
                    out_ref[1 - c, o, p, d * width : (d + 1) * width, :] = factor * total


def shape(dims):
    return jax.ShapeDtypeStruct(dims, jnp.float32)


def cost(flops, size):
    return pl.CostEstimate(flops=flops, bytes_accessed=size, transcendentals=0)


def per_device(wave, potential, occupations, centres, species, projectors, coupling):
    _, orbitals, planes, extent, _ = wave.shape
    kind_count, box, proj_count, _ = projectors.shape
    atom_count = species.shape[0]
    count = lax.axis_size("grid")
    rows = 2 * orbitals
    width = extent // count
    lanes = proj_count * box
    size = wave.size * 4
    matrix = second_derivative(extent)
    kinds = species.reshape(1, atom_count)
    send, density_term = pl.pallas_call(
        pack_kernel,
        out_shape=(shape((count, rows, width * planes, extent)), shape((planes, extent, extent))),
        in_specs=[VMEM, SMEM],
        out_specs=(VMEM, VMEM),
        compiler_params=params(),
        cost_estimate=cost(wave.size, 2 * size),
        name="pack",
    )(wave, occupations)
    held = lax.all_to_all(send, "grid", 0, 0, tiled=True)
    density = lax.psum_scatter(density_term, "orb", scatter_dimension=1, tiled=True)
    table = projectors.reshape(kind_count, box, proj_count, box, box)
    table = jnp.transpose(table, (0, 1, 3, 2, 4)).reshape(kind_count, box, box, lanes)
    table = jnp.pad(table, ((0, 0), (0, 1), (0, 0), (0, 0)))
    table = table.reshape(kind_count * (box + 1), box, lanes)
    coef = pl.pallas_call(
        project_kernel,
        out_shape=shape((rows, proj_count, atom_count)),
        in_specs=[VMEM] * 4 + [SMEM] * 2,
        out_specs=VMEM,
        scratch_shapes=[
            pltpu.VMEM((rows * planes, extent + box, extent), jnp.float32),
            pltpu.VMEM((rows, atom_count, lanes), jnp.float32),
            pltpu.SMEM((atom_count + 8,), jnp.int32),
        ],
        compiler_params=params(),
        cost_estimate=cost(40 * wave.size, 20 * size),
        name="project",
    )(wave, table, coupling, kinds, centres, species)
    reach = (box + planes - 2) // planes
    coef = coef + sum(passed_along(coef, step) for hop in range(reach) for step in (hop + 1, -hop - 1))
    local = pl.pallas_call(
        local_kernel,
        out_shape=shape((rows * planes, extent + box, extent)),
        in_specs=[VMEM] * 3,
        out_specs=VMEM,
        compiler_params=params(),
        cost_estimate=cost(12 * extent * wave.size, 3 * size),
        name="local",
    )(wave, potential, matrix)
    along = pl.pallas_call(
        along_x_kernel,
        out_shape=shape(held.shape),
        in_specs=[VMEM, VMEM, pl.BlockSpec(memory_space=pl.ANY)],
        out_specs=VMEM,
        scratch_shapes=[pltpu.VMEM((extent, extent), jnp.float32)],
        compiler_params=params(),
        cost_estimate=cost(6 * extent * wave.size, 2 * size),
        name="along_x",
    )(held, matrix, coef)
    back = lax.all_to_all(along, "grid", 0, 0, tiled=True)
    local = pl.pallas_call(
        spread_kernel,
        out_shape=shape(local.shape),
        in_specs=[VMEM] * 3 + [SMEM] * 2,
        out_specs=VMEM,
        scratch_shapes=[
            pltpu.VMEM((rows, atom_count, lanes), jnp.float32),
            pltpu.SMEM((atom_count + 8,), jnp.int32),
        ],
        compiler_params=params(),
        cost_estimate=cost(40 * wave.size, 20 * size),
        name="spread",
    )(local, table, coef, centres, species)
    update = pl.pallas_call(
        finish_kernel,
        out_shape=shape(wave.shape),
        in_specs=[VMEM, VMEM],
        out_specs=VMEM,
        compiler_params=params(),
        cost_estimate=cost(4 * wave.size, 3 * size),
        name="finish",
    )(local, back)
    return (update, density)


def solution(mesh):
    placed = (
        P(None, "orb", "grid", None, None),
        P("grid", None, None),
        P("orb"),
        P(),
        P(),
        P(),
        P(),
    )
    return jax.shard_map(
        per_device,
        mesh=mesh,
        in_specs=placed,
        out_specs=(P(None, "orb", "grid", None, None), P("grid", "orb", None)),
        check_vma=False,
    )
```

```python
import math

import jax
import jax.numpy as jnp
import numpy as np
from jax import lax
from jax.experimental import pallas as pl
from jax.experimental.pallas import tpu as pltpu
from jax.sharding import PartitionSpec as P

spacing = 0.32
time_step = 0.1
highest = lax.Precision.HIGHEST
VMEM = pl.BlockSpec(memory_space=pltpu.VMEM)
SMEM = pl.BlockSpec(memory_space=pltpu.SMEM)


def passed_along(value, axis, steps):
    count = lax.axis_size(axis)
    pairs = [(source, (source + steps) % count) for source in range(count)]
    return lax.ppermute(value, axis, pairs)


def params():
    return pltpu.CompilerParams(vmem_limit_bytes=40 * 1024 * 1024)


def second_derivative(extent):
    counts = np.arange(extent)
    signed = np.where(counts < extent // 2, counts, counts - extent)
    waves = signed * (2.0 * math.pi / (extent * spacing))
    angles = (counts[:, None] * counts[None, :] % extent) * (2.0 * math.pi / extent)
    row = np.cos(angles) @ (0.5 * waves**2) / extent
    full = row[(counts[:, None] - counts[None, :]) % extent].astype(np.float32)
    high = full.astype(jnp.bfloat16)
    low = (full - high.astype(np.float32)).astype(jnp.bfloat16)
    return jnp.asarray(np.stack([high, low]))


def split(value):
    high = value.astype(jnp.bfloat16)
    low = (value - high.astype(jnp.float32)).astype(jnp.bfloat16)
    return high, low


def mul(left, right):
    def dot(a, b):
        return jnp.dot(a, b, preferred_element_type=jnp.float32)

    return dot(left[0], right[0]) + (dot(left[0], right[1]) + dot(left[1], right[0]))


def pack_kernel(wave_ref, occ_ref, send_ref, *density_refs):
    _, orbitals, planes, extent, _ = wave_ref.shape
    count = send_ref.shape[0]
    width = extent // count
    shares = len(density_refs)
    share = extent // shares
    place = lax.axis_index("orb")
    for p in range(planes):
        for k in range(shares):
            taken = pl.ds(pl.multiple_of(lax.rem(place + k, shares) * share, share), share)
            total = None
            for o in range(orbitals):
                real = wave_ref[0, o, p, taken, :]
                imag = wave_ref[1, o, p, taken, :]
                term = occ_ref[o] * (real * real + imag * imag)
                total = term if total is None else total + term
            density_refs[k][p] = total
        for c in range(2):
            for o in range(orbitals):
                for d in range(count):
                    send_ref[d, c * orbitals + o, pl.ds(p, width, stride=planes), :] = wave_ref[
                        c, o, p, d * width : (d + 1) * width, :
                    ]


def along_x_kernel(held_ref, matrix_ref, coef_ref, out_ref, lined):
    count, rows, both, extent = held_ref.shape
    planes = extent // count
    matrix = (matrix_ref[0], matrix_ref[1])
    for r in range(rows):
        for y in range(both // planes):
            block = pl.ds(y * planes, planes)
            if planes % 8 == 0:
                column = held_ref[:, r, block, :].reshape(extent, extent)
            else:
                for s in range(count):
                    lined[s * planes : (s + 1) * planes, :] = held_ref[s, r, block, :]
                column = lined[...]
            result = mul(matrix, split(column))
            if planes % 8 == 0:
                out_ref[:, r, block, :] = result.reshape(count, planes, extent)
            else:
                lined[...] = result
                for s in range(count):
                    out_ref[s, r, block, :] = lined[s * planes : (s + 1) * planes, :]


def list_hits(centres_ref, hits, extent, planes, half_box):
    first_plane = lax.axis_index("grid") * planes

    def look(atom, found):
        start = lax.rem(first_plane - centres_ref[0, atom] + (half_box + extent), extent)
        hits[found] = atom
        meets = jnp.logical_or(start < 2 * half_box, start + planes > extent)
        return found + meets.astype(jnp.int32)

    return lax.fori_loop(0, centres_ref.shape[1], look, jnp.int32(0), unroll=8)


def atom_place(centres_ref, species_ref, atom, extent, planes, box):
    half_box = box // 2
    first_plane = lax.axis_index("grid") * planes
    start_x = lax.rem(first_plane - centres_ref[0, atom] + (half_box + extent), extent)
    start_y = lax.rem(centres_ref[1, atom] + (extent - half_box), extent)
    start_z = lax.rem(centres_ref[2, atom] + (extent - half_box), extent)
    slots = []
    for p in range(planes):
        depth = lax.rem(start_x + p, extent)
        slots.append(species_ref[atom] * (box + 1) + jnp.minimum(depth, box))
    return slots, start_y, start_z


def project_kernel(
    wave_ref,
    table_ref,
    coupling_ref,
    kinds_ref,
    centres_ref,
    species_ref,
    coef_ref,
    padded,
    sums,
    hits,
):
    _, orbitals, planes, extent, _ = wave_ref.shape
    box = table_ref.shape[1]
    lanes = table_ref.shape[2]
    rows = 2 * orbitals
    for c in range(2):
        for o in range(orbitals):
            for p in range(planes):
                at = (c * orbitals + o) * planes + p
                padded[at, :extent, :] = wave_ref[c, o, p]
                padded[at, extent:, :] = wave_ref[c, o, p, :box, :]
    sums[...] = jnp.zeros_like(sums)
    found = list_hits(centres_ref, hits, extent, planes, box // 2)
    lane = lax.broadcasted_iota(jnp.int32, (box, lanes), 1) % box

    def one(step, carry):
        atom = hits[step]
        slots, start_y, start_z = atom_place(
            centres_ref, species_ref, atom, extent, planes, box
        )
        places = lane + start_z
        places = jnp.where(places >= extent, places - extent, places)
        totals = [None] * rows
        for p in range(planes):
            beta = table_ref[slots[p]]
            for r in range(rows):
                window = padded[r * planes + p, pl.ds(start_y, box), :]
                spread_out = jnp.take_along_axis(window, places, axis=1, mode="promise_in_bounds")
                term = spread_out * beta
                totals[r] = term if totals[r] is None else totals[r] + term
        for r in range(rows):
            sums[r, pl.ds(atom, 1), :] = jnp.sum(totals[r], axis=0, keepdims=True)
        return carry

    lax.fori_loop(0, found, one, 0)
    proj_count = lanes // box
    group = lax.broadcasted_iota(jnp.int32, (proj_count, lanes), 1) // box
    member = (group == lax.broadcasted_iota(jnp.int32, (proj_count, lanes), 0)).astype(jnp.float32)
    kinds = kinds_ref[...]
    for r in range(rows):
        partial = lax.dot_general(
            member,
            sums[r],
            (((1,), (1,)), ((), ())),
            precision=highest,
            preferred_element_type=jnp.float32,
        )
        scaled = None
        for s in range(coupling_ref.shape[0]):
            term = jnp.dot(
                coupling_ref[s], partial, precision=highest, preferred_element_type=jnp.float32
            )
            term = jnp.where(kinds == s, term, 0.0)
            scaled = term if scaled is None else scaled + term
        coef_ref[r] = scaled


def local_kernel(wave_ref, potential_ref, matrix_ref, out_ref):
    _, orbitals, planes, extent, _ = wave_ref.shape
    box = out_ref.shape[1] - extent
    matrix = (matrix_ref[0], matrix_ref[1])
    for c in range(2):
        for o in range(orbitals):
            for p in range(planes):
                at = (c * orbitals + o) * planes + p
                value = wave_ref[c, o, p]
                parts = split(value)
                out_ref[at, :extent, :] = (
                    mul(matrix, parts) + mul(parts, matrix) + potential_ref[p] * value
                )
                out_ref[at, extent:, :] = jnp.zeros((box, extent), jnp.float32)


def spread_kernel(local_ref, table_ref, coef_ref, centres_ref, species_ref, out_ref, factors, hits):
    box = table_ref.shape[1]
    lanes = table_ref.shape[2]
    extent = local_ref.shape[2]
    rows = coef_ref.shape[0]
    planes = local_ref.shape[0] // rows
    proj_count = lanes // box
    group = lax.broadcasted_iota(jnp.int32, (proj_count, lanes), 1) // box
    member = (group == lax.broadcasted_iota(jnp.int32, (proj_count, lanes), 0)).astype(jnp.float32)
    for r in range(rows):
        factors[r] = lax.dot_general(
            coef_ref[r],
            member,
            (((0,), (0,)), ((), ())),
            precision=highest,
            preferred_element_type=jnp.float32,
        )
    out_ref[...] = local_ref[...]
    found = list_hits(centres_ref, hits, extent, planes, box // 2)
    lane = lax.broadcasted_iota(jnp.int32, (box, extent), 1)

    def one(step, carry):
        atom = hits[step]
        slots, start_y, start_z = atom_place(
            centres_ref, species_ref, atom, extent, planes, box
        )
        away = lane - start_z
        inside = jnp.where(away < 0, away + extent, away) < box
        turn = lax.rem(start_z, box)
        factor = [factors[r, pl.ds(atom, 1), :] for r in range(rows)]
        for p in range(planes):
            beta = table_ref[slots[p]]
            for r in range(rows):
                term = beta * factor[r]
                reach = lanes // 2
                while reach >= box:
                    term = term + pltpu.roll(term, reach, 1)
                    reach //= 2
                term = jnp.where(inside, pltpu.roll(term, turn, 1), 0.0)
                out_ref[r * planes + p, pl.ds(start_y, box), :] += term
        return carry

    lax.fori_loop(0, found, one, 0)


def finish_kernel(local_ref, along_ref, *refs):
    terms, out_ref, density_ref = refs[:-2], refs[-2], refs[-1]
    _, orbitals, planes, extent, _ = out_ref.shape
    count = along_ref.shape[0]
    width = extent // count
    box = local_ref.shape[1] - extent
    density = terms[0][...]
    for term in terms[1:]:
        density = density + term[...]
    density_ref[...] = density
    half_step = 0.5 * time_step
    for c in range(2):
        factor = half_step if c == 1 else -half_step
        for o in range(orbitals):
            r = c * orbitals + o
            for p in range(planes):
                for d in range(count):
                    total = (
                        local_ref[r * planes + p, d * width : (d + 1) * width, :]
                        + along_ref[d, r, pl.ds(p, width, stride=planes), :]
                    )
                    if d * width < box:
                        total += local_ref[
                            r * planes + p, extent + d * width : extent + (d + 1) * width, :
                        ]
                    out_ref[1 - c, o, p, d * width : (d + 1) * width, :] = factor * total


def shape(dims):
    return jax.ShapeDtypeStruct(dims, jnp.float32)


def cost(flops, size):
    return pl.CostEstimate(flops=flops, bytes_accessed=size, transcendentals=0)


def per_device(wave, potential, occupations, centres, species, projectors, coupling):
    _, orbitals, planes, extent, _ = wave.shape
    kind_count, box, proj_count, _ = projectors.shape
    atom_count = species.shape[0]
    count = lax.axis_size("grid")
    rows = 2 * orbitals
    width = extent // count
    lanes = proj_count * box
    size = wave.size * 4
    matrix = second_derivative(extent)
    kinds = species.reshape(1, atom_count)
    shares = lax.axis_size("orb")
    density_shape = shape((planes, extent // shares, extent))
    send, *terms = pl.pallas_call(
        pack_kernel,
        out_shape=[shape((count, rows, width * planes, extent))] + [density_shape] * shares,
        in_specs=[VMEM, SMEM],
        out_specs=[VMEM] * (shares + 1),
        compiler_params=params(),
        cost_estimate=cost(wave.size, 2 * size),
        name="pack",
    )(wave, occupations)
    held = lax.all_to_all(send, "grid", 0, 0, tiled=True)
    terms = [terms[0]] + [passed_along(terms[k], "orb", k) for k in range(1, shares)]
    table = projectors.reshape(kind_count, box, proj_count, box, box)
    table = jnp.transpose(table, (0, 1, 3, 2, 4)).reshape(kind_count, box, box, lanes)
    table = jnp.pad(table, ((0, 0), (0, 1), (0, 0), (0, 0)))
    table = table.reshape(kind_count * (box + 1), box, lanes)
    coef = pl.pallas_call(
        project_kernel,
        out_shape=shape((rows, proj_count, atom_count)),
        in_specs=[VMEM] * 4 + [SMEM] * 2,
        out_specs=VMEM,
        scratch_shapes=[
            pltpu.VMEM((rows * planes, extent + box, extent), jnp.float32),
            pltpu.VMEM((rows, atom_count, lanes), jnp.float32),
            pltpu.SMEM((atom_count + 8,), jnp.int32),
        ],
        compiler_params=params(),
        cost_estimate=cost(40 * wave.size, 20 * size),
        name="project",
    )(wave, table, coupling, kinds, centres, species)
    reach = (box + planes - 2) // planes
    coef = coef + sum(
        passed_along(coef, "grid", step) for hop in range(reach) for step in (hop + 1, -hop - 1)
    )
    local = pl.pallas_call(
        local_kernel,
        out_shape=shape((rows * planes, extent + box, extent)),
        in_specs=[VMEM] * 3,
        out_specs=VMEM,
        compiler_params=params(),
        cost_estimate=cost(12 * extent * wave.size, 3 * size),
        name="local",
    )(wave, potential, matrix)
    along = pl.pallas_call(
        along_x_kernel,
        out_shape=shape(held.shape),
        in_specs=[VMEM, VMEM, pl.BlockSpec(memory_space=pl.ANY)],
        out_specs=VMEM,
        scratch_shapes=[pltpu.VMEM((extent, extent), jnp.float32)],
        compiler_params=params(),
        cost_estimate=cost(6 * extent * wave.size, 2 * size),
        name="along_x",
    )(held, matrix, coef)
    back = lax.all_to_all(along, "grid", 0, 0, tiled=True)
    local = pl.pallas_call(
        spread_kernel,
        out_shape=shape(local.shape),
        in_specs=[VMEM] * 3 + [SMEM] * 2,
        out_specs=VMEM,
        scratch_shapes=[
            pltpu.VMEM((rows, atom_count, lanes), jnp.float32),
            pltpu.SMEM((atom_count + 8,), jnp.int32),
        ],
        compiler_params=params(),
        cost_estimate=cost(40 * wave.size, 20 * size),
        name="spread",
    )(local, table, coef, centres, species)
    return pl.pallas_call(
        finish_kernel,
        out_shape=(shape(wave.shape), density_shape),
        in_specs=[VMEM] * (2 + shares),
        out_specs=(VMEM, VMEM),
        compiler_params=params(),
        cost_estimate=cost(4 * wave.size, 3 * size),
        name="finish",
    )(local, back, *terms)


def solution(mesh):
    placed = (
        P(None, "orb", "grid", None, None),
        P("grid", None, None),
        P("orb"),
        P(),
        P(),
        P(),
        P(),
    )
    return jax.shard_map(
        per_device,
        mesh=mesh,
        in_specs=placed,
        out_specs=(P(None, "orb", "grid", None, None), P("grid", "orb", None)),
        check_vma=False,
    )
```

```python
import math

import jax
import jax.numpy as jnp
import numpy as np
from jax import lax
from jax.experimental import pallas as pl
from jax.experimental.pallas import tpu as pltpu
from jax.sharding import PartitionSpec as P

spacing = 0.32
time_step = 0.1
highest = lax.Precision.HIGHEST
VMEM = pl.BlockSpec(memory_space=pltpu.VMEM)
SMEM = pl.BlockSpec(memory_space=pltpu.SMEM)


def passed_along(value, axis, steps):
    count = lax.axis_size(axis)
    pairs = [(source, (source + steps) % count) for source in range(count)]
    return lax.ppermute(value, axis, pairs)


def params():
    return pltpu.CompilerParams(vmem_limit_bytes=40 * 1024 * 1024)


def second_derivative(extent):
    counts = np.arange(extent)
    signed = np.where(counts < extent // 2, counts, counts - extent)
    waves = signed * (2.0 * math.pi / (extent * spacing))
    angles = (counts[:, None] * counts[None, :] % extent) * (2.0 * math.pi / extent)
    row = np.cos(angles) @ (0.5 * waves**2) / extent
    full = row[(counts[:, None] - counts[None, :]) % extent].astype(np.float32)
    high = full.astype(jnp.bfloat16)
    low = (full - high.astype(np.float32)).astype(jnp.bfloat16)
    return jnp.asarray(np.stack([high, low]))


def split(value):
    high = value.astype(jnp.bfloat16)
    low = (value - high.astype(jnp.float32)).astype(jnp.bfloat16)
    return high, low


def mul(left, right):
    def dot(a, b):
        return jnp.dot(a, b, preferred_element_type=jnp.float32)

    return dot(left[0], right[0]) + (dot(left[0], right[1]) + dot(left[1], right[0]))


def pack_kernel(wave_ref, send_ref):
    _, orbitals, planes, extent, _ = wave_ref.shape
    count = send_ref.shape[0]
    width = extent // count
    for p in range(planes):
        for c in range(2):
            for o in range(orbitals):
                for d in range(count):
                    send_ref[d, c * orbitals + o, pl.ds(p, width, stride=planes), :] = wave_ref[
                        c, o, p, d * width : (d + 1) * width, :
                    ]


def along_x_kernel(held_ref, matrix_ref, coef_ref, out_ref, lined):
    count, rows, both, extent = held_ref.shape
    planes = extent // count
    matrix = (matrix_ref[0], matrix_ref[1])
    for r in range(rows):
        for y in range(both // planes):
            block = pl.ds(y * planes, planes)
            if planes % 8 == 0:
                column = held_ref[:, r, block, :].reshape(extent, extent)
            else:
                for s in range(count):
                    lined[s * planes : (s + 1) * planes, :] = held_ref[s, r, block, :]
                column = lined[...]
            result = mul(matrix, split(column))
            if planes % 8 == 0:
                out_ref[:, r, block, :] = result.reshape(count, planes, extent)
            else:
                lined[...] = result
                for s in range(count):
                    out_ref[s, r, block, :] = lined[s * planes : (s + 1) * planes, :]


def list_hits(centres_ref, hits, extent, planes, half_box):
    first_plane = lax.axis_index("grid") * planes

    def look(atom, found):
        start = lax.rem(first_plane - centres_ref[0, atom] + (half_box + extent), extent)
        hits[found] = atom
        meets = jnp.logical_or(start < 2 * half_box, start + planes > extent)
        return found + meets.astype(jnp.int32)

    return lax.fori_loop(0, centres_ref.shape[1], look, jnp.int32(0), unroll=8)


def atom_place(centres_ref, species_ref, atom, extent, planes, box):
    half_box = box // 2
    first_plane = lax.axis_index("grid") * planes
    start_x = lax.rem(first_plane - centres_ref[0, atom] + (half_box + extent), extent)
    start_y = lax.rem(centres_ref[1, atom] + (extent - half_box), extent)
    start_z = lax.rem(centres_ref[2, atom] + (extent - half_box), extent)
    slots = []
    for p in range(planes):
        depth = lax.rem(start_x + p, extent)
        slots.append(species_ref[atom] * (box + 1) + jnp.minimum(depth, box))
    return slots, start_y, start_z


def project_kernel(
    wave_ref,
    table_ref,
    coupling_ref,
    kinds_ref,
    centres_ref,
    species_ref,
    coef_ref,
    padded,
    sums,
    hits,
):
    _, orbitals, planes, extent, _ = wave_ref.shape
    box = table_ref.shape[1]
    lanes = table_ref.shape[2]
    rows = 2 * orbitals
    for c in range(2):
        for o in range(orbitals):
            for p in range(planes):
                at = (c * orbitals + o) * planes + p
                padded[at, :extent, :] = wave_ref[c, o, p]
                padded[at, extent:, :] = wave_ref[c, o, p, :box, :]
    sums[...] = jnp.zeros_like(sums)
    found = list_hits(centres_ref, hits, extent, planes, box // 2)
    lane = lax.broadcasted_iota(jnp.int32, (box, lanes), 1) % box

    def one(step, carry):
        atom = hits[step]
        slots, start_y, start_z = atom_place(
            centres_ref, species_ref, atom, extent, planes, box
        )
        places = lane + start_z
        places = jnp.where(places >= extent, places - extent, places)
        totals = [None] * rows
        for p in range(planes):
            beta = table_ref[slots[p]]
            for r in range(rows):
                window = padded[r * planes + p, pl.ds(start_y, box), :]
                spread_out = jnp.take_along_axis(window, places, axis=1, mode="promise_in_bounds")
                term = spread_out * beta
                totals[r] = term if totals[r] is None else totals[r] + term
        for r in range(rows):
            sums[r, pl.ds(atom, 1), :] = jnp.sum(totals[r], axis=0, keepdims=True)
        return carry

    lax.fori_loop(0, found, one, 0)
    proj_count = lanes // box
    group = lax.broadcasted_iota(jnp.int32, (proj_count, lanes), 1) // box
    member = (group == lax.broadcasted_iota(jnp.int32, (proj_count, lanes), 0)).astype(jnp.float32)
    kinds = kinds_ref[...]
    for r in range(rows):
        partial = lax.dot_general(
            member,
            sums[r],
            (((1,), (1,)), ((), ())),
            precision=highest,
            preferred_element_type=jnp.float32,
        )
        scaled = None
        for s in range(coupling_ref.shape[0]):
            term = jnp.dot(
                coupling_ref[s], partial, precision=highest, preferred_element_type=jnp.float32
            )
            term = jnp.where(kinds == s, term, 0.0)
            scaled = term if scaled is None else scaled + term
        coef_ref[r] = scaled


def local_kernel(wave_ref, potential_ref, matrix_ref, occ_ref, out_ref, *density_refs):
    _, orbitals, planes, extent, _ = wave_ref.shape
    shares = len(density_refs)
    share = extent // shares
    place = lax.axis_index("orb")
    for p in range(planes):
        for k in range(shares):
            taken = pl.ds(pl.multiple_of(lax.rem(place + k, shares) * share, share), share)
            total = None
            for o in range(orbitals):
                real = wave_ref[0, o, p, taken, :]
                imag = wave_ref[1, o, p, taken, :]
                term = occ_ref[o] * (real * real + imag * imag)
                total = term if total is None else total + term
            density_refs[k][p] = total
    box = out_ref.shape[1] - extent
    matrix = (matrix_ref[0], matrix_ref[1])
    for c in range(2):
        for o in range(orbitals):
            for p in range(planes):
                at = (c * orbitals + o) * planes + p
                value = wave_ref[c, o, p]
                parts = split(value)
                out_ref[at, :extent, :] = (
                    mul(matrix, parts) + mul(parts, matrix) + potential_ref[p] * value
                )
                out_ref[at, extent:, :] = jnp.zeros((box, extent), jnp.float32)


def spread_kernel(local_ref, table_ref, coef_ref, centres_ref, species_ref, out_ref, factors, hits):
    box = table_ref.shape[1]
    lanes = table_ref.shape[2]
    extent = local_ref.shape[2]
    rows = coef_ref.shape[0]
    planes = local_ref.shape[0] // rows
    proj_count = lanes // box
    group = lax.broadcasted_iota(jnp.int32, (proj_count, lanes), 1) // box
    member = (group == lax.broadcasted_iota(jnp.int32, (proj_count, lanes), 0)).astype(jnp.float32)
    for r in range(rows):
        factors[r] = lax.dot_general(
            coef_ref[r],
            member,
            (((0,), (0,)), ((), ())),
            precision=highest,
            preferred_element_type=jnp.float32,
        )
    out_ref[...] = local_ref[...]
    found = list_hits(centres_ref, hits, extent, planes, box // 2)
    lane = lax.broadcasted_iota(jnp.int32, (box, extent), 1)

    def one(step, carry):
        atom = hits[step]
        slots, start_y, start_z = atom_place(
            centres_ref, species_ref, atom, extent, planes, box
        )
        away = lane - start_z
        inside = jnp.where(away < 0, away + extent, away) < box
        turn = lax.rem(start_z, box)
        factor = [factors[r, pl.ds(atom, 1), :] for r in range(rows)]
        for p in range(planes):
            beta = table_ref[slots[p]]
            for r in range(rows):
                term = beta * factor[r]
                reach = lanes // 2
                while reach >= box:
                    term = term + pltpu.roll(term, reach, 1)
                    reach //= 2
                term = jnp.where(inside, pltpu.roll(term, turn, 1), 0.0)
                out_ref[r * planes + p, pl.ds(start_y, box), :] += term
        return carry

    lax.fori_loop(0, found, one, 0)


def finish_kernel(local_ref, along_ref, out_ref):
    _, orbitals, planes, extent, _ = out_ref.shape
    count = along_ref.shape[0]
    width = extent // count
    box = local_ref.shape[1] - extent
    half_step = 0.5 * time_step
    for c in range(2):
        factor = half_step if c == 1 else -half_step
        for o in range(orbitals):
            r = c * orbitals + o
            for p in range(planes):
                for d in range(count):
                    total = (
                        local_ref[r * planes + p, d * width : (d + 1) * width, :]
                        + along_ref[d, r, pl.ds(p, width, stride=planes), :]
                    )
                    if d * width < box:
                        total += local_ref[
                            r * planes + p, extent + d * width : extent + (d + 1) * width, :
                        ]
                    out_ref[1 - c, o, p, d * width : (d + 1) * width, :] = factor * total


def shape(dims):
    return jax.ShapeDtypeStruct(dims, jnp.float32)


def cost(flops, size):
    return pl.CostEstimate(flops=flops, bytes_accessed=size, transcendentals=0)


def per_device(wave, potential, occupations, centres, species, projectors, coupling):
    _, orbitals, planes, extent, _ = wave.shape
    kind_count, box, proj_count, _ = projectors.shape
    atom_count = species.shape[0]
    count = lax.axis_size("grid")
    rows = 2 * orbitals
    width = extent // count
    lanes = proj_count * box
    size = wave.size * 4
    matrix = second_derivative(extent)
    kinds = species.reshape(1, atom_count)
    shares = lax.axis_size("orb")
    density_shape = shape((planes, extent // shares, extent))
    send = pl.pallas_call(
        pack_kernel,
        out_shape=shape((count, rows, width * planes, extent)),
        in_specs=[VMEM],
        out_specs=VMEM,
        compiler_params=params(),
        cost_estimate=cost(wave.size, 2 * size),
        name="pack",
    )(wave)
    held = lax.all_to_all(send, "grid", 0, 0, tiled=True)
    table = projectors.reshape(kind_count, box, proj_count, box, box)
    table = jnp.transpose(table, (0, 1, 3, 2, 4)).reshape(kind_count, box, box, lanes)
    table = jnp.pad(table, ((0, 0), (0, 1), (0, 0), (0, 0)))
    table = table.reshape(kind_count * (box + 1), box, lanes)
    coef = pl.pallas_call(
        project_kernel,
        out_shape=shape((rows, proj_count, atom_count)),
        in_specs=[VMEM] * 4 + [SMEM] * 2,
        out_specs=VMEM,
        scratch_shapes=[
            pltpu.VMEM((rows * planes, extent + box, extent), jnp.float32),
            pltpu.VMEM((rows, atom_count, lanes), jnp.float32),
            pltpu.SMEM((atom_count + 8,), jnp.int32),
        ],
        compiler_params=params(),
        cost_estimate=cost(40 * wave.size, 20 * size),
        name="project",
    )(wave, table, coupling, kinds, centres, species)
    reach = (box + planes - 2) // planes
    own_coef = coef
    coef = coef + sum(
        passed_along(coef, "grid", step) for hop in range(reach) for step in (hop + 1, -hop - 1)
    )
    local, *terms = pl.pallas_call(
        local_kernel,
        out_shape=[shape((rows * planes, extent + box, extent))] + [density_shape] * shares,
        in_specs=[VMEM] * 3 + [SMEM],
        out_specs=[VMEM] * (shares + 1),
        compiler_params=params(),
        cost_estimate=cost(12 * extent * wave.size, 3 * size),
        name="local",
    )(wave, potential, matrix, occupations)
    density = terms[0]
    for k in range(1, shares):
        density = density + passed_along(terms[k], "orb", k)
    along = pl.pallas_call(
        along_x_kernel,
        out_shape=shape(held.shape),
        in_specs=[VMEM, VMEM, pl.BlockSpec(memory_space=pl.ANY)],
        out_specs=VMEM,
        scratch_shapes=[pltpu.VMEM((extent, extent), jnp.float32)],
        compiler_params=params(),
        cost_estimate=cost(6 * extent * wave.size, 2 * size),
        name="along_x",
    )(held, matrix, own_coef)
    back = lax.all_to_all(along, "grid", 0, 0, tiled=True)
    local = pl.pallas_call(
        spread_kernel,
        out_shape=shape(local.shape),
        in_specs=[VMEM] * 3 + [SMEM] * 2,
        out_specs=VMEM,
        scratch_shapes=[
            pltpu.VMEM((rows, atom_count, lanes), jnp.float32),
            pltpu.SMEM((atom_count + 8,), jnp.int32),
        ],
        compiler_params=params(),
        cost_estimate=cost(40 * wave.size, 20 * size),
        name="spread",
    )(local, table, coef, centres, species)
    update = pl.pallas_call(
        finish_kernel,
        out_shape=shape(wave.shape),
        in_specs=[VMEM, VMEM],
        out_specs=VMEM,
        compiler_params=params(),
        cost_estimate=cost(4 * wave.size, 3 * size),
        name="finish",
    )(local, back)
    return (update, density)


def solution(mesh):
    placed = (
        P(None, "orb", "grid", None, None),
        P("grid", None, None),
        P("orb"),
        P(),
        P(),
        P(),
        P(),
    )
    return jax.shard_map(
        per_device,
        mesh=mesh,
        in_specs=placed,
        out_specs=(P(None, "orb", "grid", None, None), P("grid", "orb", None)),
        check_vma=False,
    )
```

```python
import math

import jax
import jax.numpy as jnp
import numpy as np
from jax import lax
from jax.experimental import pallas as pl
from jax.experimental.pallas import tpu as pltpu
from jax.sharding import PartitionSpec as P

spacing = 0.32
time_step = 0.1
highest = lax.Precision.HIGHEST
VMEM = pl.BlockSpec(memory_space=pltpu.VMEM)
SMEM = pl.BlockSpec(memory_space=pltpu.SMEM)


def passed_along(value, axis, steps):
    count = lax.axis_size(axis)
    pairs = [(source, (source + steps) % count) for source in range(count)]
    return lax.ppermute(value, axis, pairs)


def params():
    return pltpu.CompilerParams(vmem_limit_bytes=40 * 1024 * 1024)


def second_derivative(extent):
    counts = np.arange(extent)
    signed = np.where(counts < extent // 2, counts, counts - extent)
    waves = signed * (2.0 * math.pi / (extent * spacing))
    angles = (counts[:, None] * counts[None, :] % extent) * (2.0 * math.pi / extent)
    row = np.cos(angles) @ (0.5 * waves**2) / extent
    full = row[(counts[:, None] - counts[None, :]) % extent].astype(np.float32)
    high = full.astype(jnp.bfloat16)
    low = (full - high.astype(np.float32)).astype(jnp.bfloat16)
    return jnp.asarray(np.stack([high, low]))


def split(value):
    high = value.astype(jnp.bfloat16)
    low = (value - high.astype(jnp.float32)).astype(jnp.bfloat16)
    return high, low


def mul(left, right):
    def dot(a, b):
        return jnp.dot(a, b, preferred_element_type=jnp.float32)

    return dot(left[0], right[0]) + (dot(left[0], right[1]) + dot(left[1], right[0]))


def pack_kernel(wave_ref, send_ref):
    _, orbitals, planes, extent, _ = wave_ref.shape
    count = send_ref.shape[0]
    width = extent // count
    for p in range(planes):
        for c in range(2):
            for o in range(orbitals):
                for d in range(count):
                    send_ref[d, c * orbitals + o, pl.ds(p, width, stride=planes), :] = wave_ref[
                        c, o, p, d * width : (d + 1) * width, :
                    ]


def along_x_kernel(held_ref, matrix_ref, coef_ref, out_ref, lined):
    count, rows, both, extent = held_ref.shape
    planes = extent // count
    matrix = (matrix_ref[0], matrix_ref[1])
    for r in range(rows):
        for y in range(both // planes):
            block = pl.ds(y * planes, planes)
            if planes % 8 == 0:
                column = held_ref[:, r, block, :].reshape(extent, extent)
            else:
                for s in range(count):
                    lined[s * planes : (s + 1) * planes, :] = held_ref[s, r, block, :]
                column = lined[...]
            result = mul(matrix, split(column))
            if planes % 8 == 0:
                out_ref[:, r, block, :] = result.reshape(count, planes, extent)
            else:
                lined[...] = result
                for s in range(count):
                    out_ref[s, r, block, :] = lined[s * planes : (s + 1) * planes, :]


def list_hits(centres_ref, hits, extent, planes, half_box):
    first_plane = lax.axis_index("grid") * planes

    def look(atom, found):
        start = lax.rem(first_plane - centres_ref[0, atom] + (half_box + extent), extent)
        hits[found] = atom
        meets = jnp.logical_or(start < 2 * half_box, start + planes > extent)
        return found + meets.astype(jnp.int32)

    return lax.fori_loop(0, centres_ref.shape[1], look, jnp.int32(0), unroll=8)


def atom_place(centres_ref, species_ref, atom, extent, planes, box):
    half_box = box // 2
    first_plane = lax.axis_index("grid") * planes
    start_x = lax.rem(first_plane - centres_ref[0, atom] + (half_box + extent), extent)
    start_y = lax.rem(centres_ref[1, atom] + (extent - half_box), extent)
    start_z = lax.rem(centres_ref[2, atom] + (extent - half_box), extent)
    slots = []
    for p in range(planes):
        depth = lax.rem(start_x + p, extent)
        slots.append(species_ref[atom] * (box + 1) + jnp.minimum(depth, box))
    return slots, start_y, start_z


def project_kernel(
    wave_ref,
    table_ref,
    coupling_ref,
    kinds_ref,
    centres_ref,
    species_ref,
    coef_ref,
    padded,
    sums,
    hits,
):
    _, orbitals, planes, extent, _ = wave_ref.shape
    box = table_ref.shape[1]
    lanes = table_ref.shape[2]
    rows = 2 * orbitals
    for c in range(2):
        for o in range(orbitals):
            for p in range(planes):
                at = (c * orbitals + o) * planes + p
                padded[at, :extent, :] = wave_ref[c, o, p]
                padded[at, extent:, :] = wave_ref[c, o, p, :box, :]
    sums[...] = jnp.zeros_like(sums)
    found = list_hits(centres_ref, hits, extent, planes, box // 2)
    lane = lax.broadcasted_iota(jnp.int32, (box, lanes), 1) % box

    def one(step, carry):
        atom = hits[step]
        slots, start_y, start_z = atom_place(
            centres_ref, species_ref, atom, extent, planes, box
        )
        places = lane + start_z
        places = jnp.where(places >= extent, places - extent, places)
        totals = [None] * rows
        for p in range(planes):
            beta = table_ref[slots[p]]
            for r in range(rows):
                window = padded[r * planes + p, pl.ds(start_y, box), :]
                spread_out = jnp.take_along_axis(window, places, axis=1, mode="promise_in_bounds")
                term = spread_out * beta
                totals[r] = term if totals[r] is None else totals[r] + term
        for r in range(rows):
            sums[r, pl.ds(atom, 1), :] = jnp.sum(totals[r], axis=0, keepdims=True)
        return carry

    lax.fori_loop(0, found, one, 0)
    proj_count = lanes // box
    group = lax.broadcasted_iota(jnp.int32, (proj_count, lanes), 1) // box
    member = (group == lax.broadcasted_iota(jnp.int32, (proj_count, lanes), 0)).astype(jnp.float32)
    kinds = kinds_ref[...]
    for r in range(rows):
        partial = lax.dot_general(
            member,
            sums[r],
            (((1,), (1,)), ((), ())),
            precision=highest,
            preferred_element_type=jnp.float32,
        )
        scaled = None
        for s in range(coupling_ref.shape[0]):
            term = jnp.dot(
                coupling_ref[s], partial, precision=highest, preferred_element_type=jnp.float32
            )
            term = jnp.where(kinds == s, term, 0.0)
            scaled = term if scaled is None else scaled + term
        coef_ref[r] = scaled


def local_kernel(wave_ref, potential_ref, matrix_ref, occ_ref, out_ref, *density_refs):
    _, orbitals, planes, extent, _ = wave_ref.shape
    shares = len(density_refs)
    share = extent // shares
    place = lax.axis_index("orb")
    for p in range(planes):
        for k in range(shares):
            taken = pl.ds(pl.multiple_of(lax.rem(place + k, shares) * share, share), share)
            total = None
            for o in range(orbitals):
                real = wave_ref[0, o, p, taken, :]
                imag = wave_ref[1, o, p, taken, :]
                term = occ_ref[o] * (real * real + imag * imag)
                total = term if total is None else total + term
            density_refs[k][p] = total
    box = out_ref.shape[1] - extent
    matrix = (matrix_ref[0], matrix_ref[1])
    for c in range(2):
        for o in range(orbitals):
            for p in range(planes):
                at = (c * orbitals + o) * planes + p
                value = wave_ref[c, o, p]
                parts = split(value)
                out_ref[at, :extent, :] = (
                    mul(matrix, parts) + mul(parts, matrix) + potential_ref[p] * value
                )
                out_ref[at, extent:, :] = jnp.zeros((box, extent), jnp.float32)


def spread_kernel(local_ref, table_ref, coef_ref, centres_ref, species_ref, out_ref, factors, hits):
    box = table_ref.shape[1]
    lanes = table_ref.shape[2]
    extent = local_ref.shape[2]
    rows = coef_ref.shape[0]
    planes = local_ref.shape[0] // rows
    proj_count = lanes // box
    group = lax.broadcasted_iota(jnp.int32, (proj_count, lanes), 1) // box
    member = (group == lax.broadcasted_iota(jnp.int32, (proj_count, lanes), 0)).astype(jnp.float32)
    for r in range(rows):
        factors[r] = lax.dot_general(
            coef_ref[r],
            member,
            (((0,), (0,)), ((), ())),
            precision=highest,
            preferred_element_type=jnp.float32,
        )
    out_ref[...] = local_ref[...]
    found = list_hits(centres_ref, hits, extent, planes, box // 2)
    lane = lax.broadcasted_iota(jnp.int32, (box, extent), 1)

    def one(step, carry):
        atom = hits[step]
        slots, start_y, start_z = atom_place(
            centres_ref, species_ref, atom, extent, planes, box
        )
        away = lane - start_z
        inside = jnp.where(away < 0, away + extent, away) < box
        turn = lax.rem(start_z, box)
        factor = [factors[r, pl.ds(atom, 1), :] for r in range(rows)]
        for p in range(planes):
            beta = table_ref[slots[p]]
            for r in range(rows):
                term = beta * factor[r]
                reach = lanes // 2
                while reach >= box:
                    term = term + pltpu.roll(term, reach, 1)
                    reach //= 2
                term = jnp.where(inside, pltpu.roll(term, turn, 1), 0.0)
                out_ref[r * planes + p, pl.ds(start_y, box), :] += term
        return carry

    lax.fori_loop(0, found, one, 0)


def finish_kernel(local_ref, along_ref, out_ref):
    _, orbitals, planes, extent, _ = out_ref.shape
    count = along_ref.shape[0]
    width = extent // count
    box = local_ref.shape[1] - extent
    half_step = 0.5 * time_step
    for c in range(2):
        factor = half_step if c == 1 else -half_step
        for o in range(orbitals):
            r = c * orbitals + o
            for p in range(planes):
                for d in range(count):
                    total = (
                        local_ref[r * planes + p, d * width : (d + 1) * width, :]
                        + along_ref[d, r, pl.ds(p, width, stride=planes), :]
                    )
                    if d * width < box:
                        total += local_ref[
                            r * planes + p, extent + d * width : extent + (d + 1) * width, :
                        ]
                    out_ref[1 - c, o, p, d * width : (d + 1) * width, :] = factor * total


def shape(dims):
    return jax.ShapeDtypeStruct(dims, jnp.float32)


def cost(flops, size):
    return pl.CostEstimate(flops=flops, bytes_accessed=size, transcendentals=0)


def per_device(wave, potential, occupations, centres, species, projectors, coupling):
    _, orbitals, planes, extent, _ = wave.shape
    kind_count, box, proj_count, _ = projectors.shape
    atom_count = species.shape[0]
    count = lax.axis_size("grid")
    rows = 2 * orbitals
    width = extent // count
    lanes = proj_count * box
    size = wave.size * 4
    matrix = second_derivative(extent)
    kinds = species.reshape(1, atom_count)
    shares = lax.axis_size("orb")
    density_shape = shape((planes, extent // shares, extent))
    send = pl.pallas_call(
        pack_kernel,
        out_shape=shape((count, rows, width * planes, extent)),
        in_specs=[VMEM],
        out_specs=VMEM,
        compiler_params=params(),
        cost_estimate=cost(wave.size, 2 * size),
        name="pack",
    )(wave)
    held = lax.all_to_all(send, "grid", 0, 0, tiled=True)
    table = projectors.reshape(kind_count, box, proj_count, box, box)
    table = jnp.transpose(table, (0, 1, 3, 2, 4)).reshape(kind_count, box, box, lanes)
    table = jnp.pad(table, ((0, 0), (0, 1), (0, 0), (0, 0)))
    table = table.reshape(kind_count * (box + 1), box, lanes)
    coef = pl.pallas_call(
        project_kernel,
        out_shape=shape((rows, proj_count, atom_count)),
        in_specs=[VMEM] * 4 + [SMEM] * 2,
        out_specs=VMEM,
        scratch_shapes=[
            pltpu.VMEM((rows * planes, extent + box, extent), jnp.float32),
            pltpu.VMEM((rows, atom_count, lanes), jnp.float32),
            pltpu.SMEM((atom_count + 8,), jnp.int32),
        ],
        compiler_params=params(),
        cost_estimate=cost(40 * wave.size, 20 * size),
        name="project",
    )(wave, table, coupling, kinds, centres, species)
    reach = (box + planes - 2) // planes
    coef = coef + sum(
        passed_along(coef, "grid", step) for hop in range(reach) for step in (hop + 1, -hop - 1)
    )
    local, *terms = pl.pallas_call(
        local_kernel,
        out_shape=[shape((rows * planes, extent + box, extent))] + [density_shape] * shares,
        in_specs=[VMEM] * 3 + [SMEM],
        out_specs=[VMEM] * (shares + 1),
        compiler_params=params(),
        cost_estimate=cost(12 * extent * wave.size, 3 * size),
        name="local",
    )(wave, potential, matrix, occupations)
    density = terms[0]
    for k in range(1, shares):
        density = density + passed_along(terms[k], "orb", k)
    along = pl.pallas_call(
        along_x_kernel,
        out_shape=shape(held.shape),
        in_specs=[VMEM, VMEM, pl.BlockSpec(memory_space=pl.ANY)],
        out_specs=VMEM,
        scratch_shapes=[pltpu.VMEM((extent, extent), jnp.float32)],
        compiler_params=params(),
        cost_estimate=cost(6 * extent * wave.size, 2 * size),
        name="along_x",
    )(held, matrix, coef)
    back = lax.all_to_all(along, "grid", 0, 0, tiled=True)
    local = pl.pallas_call(
        spread_kernel,
        out_shape=shape(local.shape),
        in_specs=[VMEM] * 3 + [SMEM] * 2,
        out_specs=VMEM,
        scratch_shapes=[
            pltpu.VMEM((rows, atom_count, lanes), jnp.float32),
            pltpu.SMEM((atom_count + 8,), jnp.int32),
        ],
        compiler_params=params(),
        cost_estimate=cost(40 * wave.size, 20 * size),
        name="spread",
    )(local, table, coef, centres, species)
    update = pl.pallas_call(
        finish_kernel,
        out_shape=shape(wave.shape),
        in_specs=[VMEM, VMEM],
        out_specs=VMEM,
        compiler_params=params(),
        cost_estimate=cost(4 * wave.size, 3 * size),
        name="finish",
    )(local, back)
    return (update, density)


def solution(mesh):
    placed = (
        P(None, "orb", "grid", None, None),
        P("grid", None, None),
        P("orb"),
        P(),
        P(),
        P(),
        P(),
    )
    return jax.shard_map(
        per_device,
        mesh=mesh,
        in_specs=placed,
        out_specs=(P(None, "orb", "grid", None, None), P("grid", "orb", None)),
        check_vma=False,
    )
```

```python
import functools
import math

import jax
import jax.numpy as jnp
import numpy as np
from jax import lax
from jax.experimental import pallas as pl
from jax.experimental.pallas import tpu as pltpu
from jax.sharding import PartitionSpec as P

spacing = 0.32
time_step = 0.1
highest = lax.Precision.HIGHEST
VMEM = pl.BlockSpec(memory_space=pltpu.VMEM)
SMEM = pl.BlockSpec(memory_space=pltpu.SMEM)


def passed_along(value, axis, steps):
    count = lax.axis_size(axis)
    pairs = [(source, (source + steps) % count) for source in range(count)]
    return lax.ppermute(value, axis, pairs)


def params():
    return pltpu.CompilerParams(vmem_limit_bytes=40 * 1024 * 1024)


def second_derivative(extent):
    counts = np.arange(extent)
    signed = np.where(counts < extent // 2, counts, counts - extent)
    waves = signed * (2.0 * math.pi / (extent * spacing))
    angles = (counts[:, None] * counts[None, :] % extent) * (2.0 * math.pi / extent)
    row = np.cos(angles) @ (0.5 * waves**2) / extent
    full = row[(counts[:, None] - counts[None, :]) % extent].astype(np.float32)
    high = full.astype(jnp.bfloat16)
    low = (full - high.astype(np.float32)).astype(jnp.bfloat16)
    return jnp.asarray(np.stack([high, low]))


def split(value):
    high = value.astype(jnp.bfloat16)
    low = (value - high.astype(jnp.float32)).astype(jnp.bfloat16)
    return high, low


def mul(left, right):
    def dot(a, b):
        return jnp.dot(a, b, preferred_element_type=jnp.float32)

    return dot(left[0], right[0]) + (dot(left[0], right[1]) + dot(left[1], right[0]))


def pack_kernel(c, wave_ref, send_ref):
    _, orbitals, planes, extent, _ = wave_ref.shape
    count = send_ref.shape[0]
    width = extent // count
    for p in range(planes):
        for o in range(orbitals):
            for d in range(count):
                send_ref[d, o, pl.ds(p, width, stride=planes), :] = wave_ref[
                    c, o, p, d * width : (d + 1) * width, :
                ]


def along_x_kernel(held_ref, matrix_ref, coef_ref, out_ref, lined):
    count, rows, both, extent = held_ref.shape
    planes = extent // count
    matrix = (matrix_ref[0], matrix_ref[1])
    for r in range(rows):
        for y in range(both // planes):
            block = pl.ds(y * planes, planes)
            if planes % 8 == 0:
                column = held_ref[:, r, block, :].reshape(extent, extent)
            else:
                for s in range(count):
                    lined[s * planes : (s + 1) * planes, :] = held_ref[s, r, block, :]
                column = lined[...]
            result = mul(matrix, split(column))
            if planes % 8 == 0:
                out_ref[:, r, block, :] = result.reshape(count, planes, extent)
            else:
                lined[...] = result
                for s in range(count):
                    out_ref[s, r, block, :] = lined[s * planes : (s + 1) * planes, :]


def list_hits(centres_ref, hits, extent, planes, half_box):
    first_plane = lax.axis_index("grid") * planes

    def look(atom, found):
        start = lax.rem(first_plane - centres_ref[0, atom] + (half_box + extent), extent)
        hits[found] = atom
        meets = jnp.logical_or(start < 2 * half_box, start + planes > extent)
        return found + meets.astype(jnp.int32)

    return lax.fori_loop(0, centres_ref.shape[1], look, jnp.int32(0), unroll=8)


def atom_place(centres_ref, species_ref, atom, extent, planes, box):
    half_box = box // 2
    first_plane = lax.axis_index("grid") * planes
    start_x = lax.rem(first_plane - centres_ref[0, atom] + (half_box + extent), extent)
    start_y = lax.rem(centres_ref[1, atom] + (extent - half_box), extent)
    start_z = lax.rem(centres_ref[2, atom] + (extent - half_box), extent)
    slots = []
    for p in range(planes):
        depth = lax.rem(start_x + p, extent)
        slots.append(species_ref[atom] * (box + 1) + jnp.minimum(depth, box))
    return slots, start_y, start_z


def project_kernel(
    wave_ref,
    table_ref,
    coupling_ref,
    kinds_ref,
    centres_ref,
    species_ref,
    coef_ref,
    padded,
    sums,
    hits,
):
    _, orbitals, planes, extent, _ = wave_ref.shape
    box = table_ref.shape[1]
    lanes = table_ref.shape[2]
    rows = 2 * orbitals
    for c in range(2):
        for o in range(orbitals):
            for p in range(planes):
                at = (c * orbitals + o) * planes + p
                padded[at, :extent, :] = wave_ref[c, o, p]
                padded[at, extent:, :] = wave_ref[c, o, p, :box, :]
    sums[...] = jnp.zeros_like(sums)
    found = list_hits(centres_ref, hits, extent, planes, box // 2)
    lane = lax.broadcasted_iota(jnp.int32, (box, lanes), 1) % box

    def one(step, carry):
        atom = hits[step]
        slots, start_y, start_z = atom_place(
            centres_ref, species_ref, atom, extent, planes, box
        )
        places = lane + start_z
        places = jnp.where(places >= extent, places - extent, places)
        totals = [None] * rows
        for p in range(planes):
            beta = table_ref[slots[p]]
            for r in range(rows):
                window = padded[r * planes + p, pl.ds(start_y, box), :]
                spread_out = jnp.take_along_axis(window, places, axis=1, mode="promise_in_bounds")
                term = spread_out * beta
                totals[r] = term if totals[r] is None else totals[r] + term
        for r in range(rows):
            sums[r, pl.ds(atom, 1), :] = jnp.sum(totals[r], axis=0, keepdims=True)
        return carry

    lax.fori_loop(0, found, one, 0)
    proj_count = lanes // box
    group = lax.broadcasted_iota(jnp.int32, (proj_count, lanes), 1) // box
    member = (group == lax.broadcasted_iota(jnp.int32, (proj_count, lanes), 0)).astype(jnp.float32)
    kinds = kinds_ref[...]
    for r in range(rows):
        partial = lax.dot_general(
            member,
            sums[r],
            (((1,), (1,)), ((), ())),
            precision=highest,
            preferred_element_type=jnp.float32,
        )
        scaled = None
        for s in range(coupling_ref.shape[0]):
            term = jnp.dot(
                coupling_ref[s], partial, precision=highest, preferred_element_type=jnp.float32
            )
            term = jnp.where(kinds == s, term, 0.0)
            scaled = term if scaled is None else scaled + term
        coef_ref[r] = scaled


def local_kernel(wave_ref, potential_ref, matrix_ref, occ_ref, out_ref, *density_refs):
    _, orbitals, planes, extent, _ = wave_ref.shape
    shares = len(density_refs)
    share = extent // shares
    place = lax.axis_index("orb")
    for p in range(planes):
        for k in range(shares):
            taken = pl.ds(pl.multiple_of(lax.rem(place + k, shares) * share, share), share)
            total = None
            for o in range(orbitals):
                real = wave_ref[0, o, p, taken, :]
                imag = wave_ref[1, o, p, taken, :]
                term = occ_ref[o] * (real * real + imag * imag)
                total = term if total is None else total + term
            density_refs[k][p] = total
    box = out_ref.shape[1] - extent
    matrix = (matrix_ref[0], matrix_ref[1])
    for c in range(2):
        for o in range(orbitals):
            for p in range(planes):
                at = (c * orbitals + o) * planes + p
                value = wave_ref[c, o, p]
                parts = split(value)
                out_ref[at, :extent, :] = (
                    mul(matrix, parts) + mul(parts, matrix) + potential_ref[p] * value
                )
                out_ref[at, extent:, :] = jnp.zeros((box, extent), jnp.float32)


def spread_kernel(local_ref, table_ref, coef_ref, centres_ref, species_ref, out_ref, factors, hits):
    box = table_ref.shape[1]
    lanes = table_ref.shape[2]
    extent = local_ref.shape[2]
    rows = coef_ref.shape[0]
    planes = local_ref.shape[0] // rows
    proj_count = lanes // box
    group = lax.broadcasted_iota(jnp.int32, (proj_count, lanes), 1) // box
    member = (group == lax.broadcasted_iota(jnp.int32, (proj_count, lanes), 0)).astype(jnp.float32)
    for r in range(rows):
        factors[r] = lax.dot_general(
            coef_ref[r],
            member,
            (((0,), (0,)), ((), ())),
            precision=highest,
            preferred_element_type=jnp.float32,
        )
    out_ref[...] = local_ref[...]
    found = list_hits(centres_ref, hits, extent, planes, box // 2)
    lane = lax.broadcasted_iota(jnp.int32, (box, extent), 1)

    def one(step, carry):
        atom = hits[step]
        slots, start_y, start_z = atom_place(
            centres_ref, species_ref, atom, extent, planes, box
        )
        away = lane - start_z
        inside = jnp.where(away < 0, away + extent, away) < box
        turn = lax.rem(start_z, box)
        factor = [factors[r, pl.ds(atom, 1), :] for r in range(rows)]
        for p in range(planes):
            beta = table_ref[slots[p]]
            for r in range(rows):
                term = beta * factor[r]
                reach = lanes // 2
                while reach >= box:
                    term = term + pltpu.roll(term, reach, 1)
                    reach //= 2
                term = jnp.where(inside, pltpu.roll(term, turn, 1), 0.0)
                out_ref[r * planes + p, pl.ds(start_y, box), :] += term
        return carry

    lax.fori_loop(0, found, one, 0)


def finish_kernel(local_ref, real_ref, imag_ref, out_ref):
    _, orbitals, planes, extent, _ = out_ref.shape
    count = real_ref.shape[0]
    width = extent // count
    box = local_ref.shape[1] - extent
    half_step = 0.5 * time_step
    for c in range(2):
        factor = half_step if c == 1 else -half_step
        along_ref = (real_ref, imag_ref)[c]
        for o in range(orbitals):
            r = c * orbitals + o
            for p in range(planes):
                for d in range(count):
                    total = (
                        local_ref[r * planes + p, d * width : (d + 1) * width, :]
                        + along_ref[d, o, pl.ds(p, width, stride=planes), :]
                    )
                    if d * width < box:
                        total += local_ref[
                            r * planes + p, extent + d * width : extent + (d + 1) * width, :
                        ]
                    out_ref[1 - c, o, p, d * width : (d + 1) * width, :] = factor * total


def shape(dims):
    return jax.ShapeDtypeStruct(dims, jnp.float32)


def cost(flops, size):
    return pl.CostEstimate(flops=flops, bytes_accessed=size, transcendentals=0)


def per_device(wave, potential, occupations, centres, species, projectors, coupling):
    _, orbitals, planes, extent, _ = wave.shape
    kind_count, box, proj_count, _ = projectors.shape
    atom_count = species.shape[0]
    count = lax.axis_size("grid")
    rows = 2 * orbitals
    width = extent // count
    lanes = proj_count * box
    size = wave.size * 4
    matrix = second_derivative(extent)
    kinds = species.reshape(1, atom_count)
    shares = lax.axis_size("orb")
    density_shape = shape((planes, extent // shares, extent))
    held = []
    for c in range(2):
        send = pl.pallas_call(
            functools.partial(pack_kernel, c),
            out_shape=shape((count, orbitals, width * planes, extent)),
            in_specs=[VMEM],
            out_specs=VMEM,
            compiler_params=params(),
            cost_estimate=cost(wave.size, size),
            name="pack",
        )(wave)
        held.append(lax.all_to_all(send, "grid", 0, 0, tiled=True))
    table = projectors.reshape(kind_count, box, proj_count, box, box)
    table = jnp.transpose(table, (0, 1, 3, 2, 4)).reshape(kind_count, box, box, lanes)
    table = jnp.pad(table, ((0, 0), (0, 1), (0, 0), (0, 0)))
    table = table.reshape(kind_count * (box + 1), box, lanes)
    coef = pl.pallas_call(
        project_kernel,
        out_shape=shape((rows, proj_count, atom_count)),
        in_specs=[VMEM] * 4 + [SMEM] * 2,
        out_specs=VMEM,
        scratch_shapes=[
            pltpu.VMEM((rows * planes, extent + box, extent), jnp.float32),
            pltpu.VMEM((rows, atom_count, lanes), jnp.float32),
            pltpu.SMEM((atom_count + 8,), jnp.int32),
        ],
        compiler_params=params(),
        cost_estimate=cost(40 * wave.size, 20 * size),
        name="project",
    )(wave, table, coupling, kinds, centres, species)
    reach = (box + planes - 2) // planes
    own_coef = coef
    coef = coef + sum(
        passed_along(coef, "grid", step) for hop in range(reach) for step in (hop + 1, -hop - 1)
    )
    local, *terms = pl.pallas_call(
        local_kernel,
        out_shape=[shape((rows * planes, extent + box, extent))] + [density_shape] * shares,
        in_specs=[VMEM] * 3 + [SMEM],
        out_specs=[VMEM] * (shares + 1),
        compiler_params=params(),
        cost_estimate=cost(12 * extent * wave.size, 3 * size),
        name="local",
    )(wave, potential, matrix, occupations)
    density = terms[0]
    for k in range(1, shares):
        density = density + passed_along(terms[k], "orb", k)
    back = []
    for c in range(2):
        along = pl.pallas_call(
            along_x_kernel,
            out_shape=shape(held[c].shape),
            in_specs=[VMEM, VMEM, pl.BlockSpec(memory_space=pl.ANY)],
            out_specs=VMEM,
            scratch_shapes=[pltpu.VMEM((extent, extent), jnp.float32)],
            compiler_params=params(),
            cost_estimate=cost(3 * extent * wave.size, size),
            name="along_x",
        )(held[c], matrix, own_coef if c == 0 else coef)
        back.append(lax.all_to_all(along, "grid", 0, 0, tiled=True))
    local = pl.pallas_call(
        spread_kernel,
        out_shape=shape(local.shape),
        in_specs=[VMEM] * 3 + [SMEM] * 2,
        out_specs=VMEM,
        scratch_shapes=[
            pltpu.VMEM((rows, atom_count, lanes), jnp.float32),
            pltpu.SMEM((atom_count + 8,), jnp.int32),
        ],
        compiler_params=params(),
        cost_estimate=cost(40 * wave.size, 20 * size),
        name="spread",
    )(local, table, coef, centres, species)
    update = pl.pallas_call(
        finish_kernel,
        out_shape=shape(wave.shape),
        in_specs=[VMEM] * 3,
        out_specs=VMEM,
        compiler_params=params(),
        cost_estimate=cost(4 * wave.size, 3 * size),
        name="finish",
    )(local, *back)
    return (update, density)


def solution(mesh):
    placed = (
        P(None, "orb", "grid", None, None),
        P("grid", None, None),
        P("orb"),
        P(),
        P(),
        P(),
        P(),
    )
    return jax.shard_map(
        per_device,
        mesh=mesh,
        in_specs=placed,
        out_specs=(P(None, "orb", "grid", None, None), P("grid", "orb", None)),
        check_vma=False,
    )
```

```python
import functools
import math

import jax
import jax.numpy as jnp
import numpy as np
from jax import lax
from jax.experimental import pallas as pl
from jax.experimental.pallas import tpu as pltpu
from jax.sharding import PartitionSpec as P

spacing = 0.32
time_step = 0.1
highest = lax.Precision.HIGHEST
VMEM = pl.BlockSpec(memory_space=pltpu.VMEM)
SMEM = pl.BlockSpec(memory_space=pltpu.SMEM)


def passed_along(value, axis, steps):
    count = lax.axis_size(axis)
    pairs = [(source, (source + steps) % count) for source in range(count)]
    return lax.ppermute(value, axis, pairs)


def params():
    return pltpu.CompilerParams(vmem_limit_bytes=40 * 1024 * 1024)


def second_derivative(extent):
    counts = np.arange(extent)
    signed = np.where(counts < extent // 2, counts, counts - extent)
    waves = signed * (2.0 * math.pi / (extent * spacing))
    angles = (counts[:, None] * counts[None, :] % extent) * (2.0 * math.pi / extent)
    row = np.cos(angles) @ (0.5 * waves**2) / extent
    full = row[(counts[:, None] - counts[None, :]) % extent].astype(np.float32)
    high = full.astype(jnp.bfloat16)
    low = (full - high.astype(np.float32)).astype(jnp.bfloat16)
    return jnp.asarray(np.stack([high, low]))


def split(value):
    high = value.astype(jnp.bfloat16)
    low = (value - high.astype(jnp.float32)).astype(jnp.bfloat16)
    return high, low


def mul(left, right):
    def dot(a, b):
        return jnp.dot(a, b, preferred_element_type=jnp.float32)

    return dot(left[0], right[0]) + (dot(left[0], right[1]) + dot(left[1], right[0]))


def pack_kernel(planes, wave_ref, send_ref):
    _, orbitals, _, extent, _ = wave_ref.shape
    count = send_ref.shape[0]
    width = extent // count
    p = pl.program_id(0)
    for c in range(2):
        for o in range(orbitals):
            for d in range(count):
                send_ref[d, c * orbitals + o, pl.ds(p, width, stride=planes), :] = wave_ref[
                    c, o, 0, d * width : (d + 1) * width, :
                ]


def along_x_kernel(held_ref, matrix_ref, coef_ref, out_ref, lined):
    count, rows, both, extent = held_ref.shape
    planes = extent // count
    matrix = (matrix_ref[0], matrix_ref[1])
    for r in range(rows):
        for y in range(both // planes):
            block = pl.ds(y * planes, planes)
            if planes % 8 == 0:
                column = held_ref[:, r, block, :].reshape(extent, extent)
            else:
                for s in range(count):
                    lined[s * planes : (s + 1) * planes, :] = held_ref[s, r, block, :]
                column = lined[...]
            result = mul(matrix, split(column))
            if planes % 8 == 0:
                out_ref[:, r, block, :] = result.reshape(count, planes, extent)
            else:
                lined[...] = result
                for s in range(count):
                    out_ref[s, r, block, :] = lined[s * planes : (s + 1) * planes, :]


def list_hits(centres_ref, hits, extent, planes, half_box):
    first_plane = lax.axis_index("grid") * planes

    def look(atom, found):
        start = lax.rem(first_plane - centres_ref[0, atom] + (half_box + extent), extent)
        hits[found] = atom
        meets = jnp.logical_or(start < 2 * half_box, start + planes > extent)
        return found + meets.astype(jnp.int32)

    return lax.fori_loop(0, centres_ref.shape[1], look, jnp.int32(0), unroll=8)


def atom_place(centres_ref, species_ref, atom, extent, planes, box):
    half_box = box // 2
    first_plane = lax.axis_index("grid") * planes
    start_x = lax.rem(first_plane - centres_ref[0, atom] + (half_box + extent), extent)
    start_y = lax.rem(centres_ref[1, atom] + (extent - half_box), extent)
    start_z = lax.rem(centres_ref[2, atom] + (extent - half_box), extent)
    slots = []
    for p in range(planes):
        depth = lax.rem(start_x + p, extent)
        slots.append(species_ref[atom] * (box + 1) + jnp.minimum(depth, box))
    return slots, start_y, start_z


def project_kernel(
    wave_ref,
    table_ref,
    coupling_ref,
    kinds_ref,
    centres_ref,
    species_ref,
    coef_ref,
    padded,
    sums,
    hits,
):
    _, orbitals, planes, extent, _ = wave_ref.shape
    box = table_ref.shape[1]
    lanes = table_ref.shape[2]
    rows = 2 * orbitals
    for c in range(2):
        for o in range(orbitals):
            for p in range(planes):
                at = (c * orbitals + o) * planes + p
                padded[at, :extent, :] = wave_ref[c, o, p]
                padded[at, extent:, :] = wave_ref[c, o, p, :box, :]
    sums[...] = jnp.zeros_like(sums)
    found = list_hits(centres_ref, hits, extent, planes, box // 2)
    lane = lax.broadcasted_iota(jnp.int32, (box, lanes), 1) % box

    def one(step, carry):
        atom = hits[step]
        slots, start_y, start_z = atom_place(
            centres_ref, species_ref, atom, extent, planes, box
        )
        places = lane + start_z
        places = jnp.where(places >= extent, places - extent, places)
        totals = [None] * rows
        for p in range(planes):
            beta = table_ref[slots[p]]
            for r in range(rows):
                window = padded[r * planes + p, pl.ds(start_y, box), :]
                spread_out = jnp.take_along_axis(window, places, axis=1, mode="promise_in_bounds")
                term = spread_out * beta
                totals[r] = term if totals[r] is None else totals[r] + term
        for r in range(rows):
            sums[r, pl.ds(atom, 1), :] = jnp.sum(totals[r], axis=0, keepdims=True)
        return carry

    lax.fori_loop(0, found, one, 0)
    proj_count = lanes // box
    group = lax.broadcasted_iota(jnp.int32, (proj_count, lanes), 1) // box
    member = (group == lax.broadcasted_iota(jnp.int32, (proj_count, lanes), 0)).astype(jnp.float32)
    kinds = kinds_ref[...]
    for r in range(rows):
        partial = lax.dot_general(
            member,
            sums[r],
            (((1,), (1,)), ((), ())),
            precision=highest,
            preferred_element_type=jnp.float32,
        )
        scaled = None
        for s in range(coupling_ref.shape[0]):
            term = jnp.dot(
                coupling_ref[s], partial, precision=highest, preferred_element_type=jnp.float32
            )
            term = jnp.where(kinds == s, term, 0.0)
            scaled = term if scaled is None else scaled + term
        coef_ref[r] = scaled


def local_kernel(wave_ref, potential_ref, matrix_ref, occ_ref, out_ref, *density_refs):
    _, orbitals, planes, extent, _ = wave_ref.shape
    shares = len(density_refs)
    share = extent // shares
    place = lax.axis_index("orb")
    for p in range(planes):
        for k in range(shares):
            taken = pl.ds(pl.multiple_of(lax.rem(place + k, shares) * share, share), share)
            total = None
            for o in range(orbitals):
                real = wave_ref[0, o, p, taken, :]
                imag = wave_ref[1, o, p, taken, :]
                term = occ_ref[o] * (real * real + imag * imag)
                total = term if total is None else total + term
            density_refs[k][p] = total
    box = out_ref.shape[1] - extent
    matrix = (matrix_ref[0], matrix_ref[1])
    for c in range(2):
        for o in range(orbitals):
            for p in range(planes):
                at = (c * orbitals + o) * planes + p
                value = wave_ref[c, o, p]
                parts = split(value)
                out_ref[at, :extent, :] = (
                    mul(matrix, parts) + mul(parts, matrix) + potential_ref[p] * value
                )
                out_ref[at, extent:, :] = jnp.zeros((box, extent), jnp.float32)


def spread_kernel(local_ref, table_ref, coef_ref, centres_ref, species_ref, out_ref, factors, hits):
    box = table_ref.shape[1]
    lanes = table_ref.shape[2]
    extent = local_ref.shape[2]
    rows = coef_ref.shape[0]
    planes = local_ref.shape[0] // rows
    proj_count = lanes // box
    group = lax.broadcasted_iota(jnp.int32, (proj_count, lanes), 1) // box
    member = (group == lax.broadcasted_iota(jnp.int32, (proj_count, lanes), 0)).astype(jnp.float32)
    for r in range(rows):
        factors[r] = lax.dot_general(
            coef_ref[r],
            member,
            (((0,), (0,)), ((), ())),
            precision=highest,
            preferred_element_type=jnp.float32,
        )
    out_ref[...] = local_ref[...]
    found = list_hits(centres_ref, hits, extent, planes, box // 2)
    lane = lax.broadcasted_iota(jnp.int32, (box, extent), 1)

    def one(step, carry):
        atom = hits[step]
        slots, start_y, start_z = atom_place(
            centres_ref, species_ref, atom, extent, planes, box
        )
        away = lane - start_z
        inside = jnp.where(away < 0, away + extent, away) < box
        turn = lax.rem(start_z, box)
        factor = [factors[r, pl.ds(atom, 1), :] for r in range(rows)]
        for p in range(planes):
            beta = table_ref[slots[p]]
            for r in range(rows):
                term = beta * factor[r]
                reach = lanes // 2
                while reach >= box:
                    term = term + pltpu.roll(term, reach, 1)
                    reach //= 2
                term = jnp.where(inside, pltpu.roll(term, turn, 1), 0.0)
                out_ref[r * planes + p, pl.ds(start_y, box), :] += term
        return carry

    lax.fori_loop(0, found, one, 0)


def finish_kernel(local_ref, along_ref, out_ref):
    _, orbitals, planes, extent, _ = out_ref.shape
    count = along_ref.shape[0]
    width = extent // count
    box = local_ref.shape[1] - extent
    half_step = 0.5 * time_step
    for c in range(2):
        factor = half_step if c == 1 else -half_step
        for o in range(orbitals):
            r = c * orbitals + o
            for p in range(planes):
                for d in range(count):
                    total = (
                        local_ref[r * planes + p, d * width : (d + 1) * width, :]
                        + along_ref[d, r, pl.ds(p, width, stride=planes), :]
                    )
                    if d * width < box:
                        total += local_ref[
                            r * planes + p, extent + d * width : extent + (d + 1) * width, :
                        ]
                    out_ref[1 - c, o, p, d * width : (d + 1) * width, :] = factor * total


def shape(dims):
    return jax.ShapeDtypeStruct(dims, jnp.float32)


def cost(flops, size):
    return pl.CostEstimate(flops=flops, bytes_accessed=size, transcendentals=0)


def per_device(wave, potential, occupations, centres, species, projectors, coupling):
    _, orbitals, planes, extent, _ = wave.shape
    kind_count, box, proj_count, _ = projectors.shape
    atom_count = species.shape[0]
    count = lax.axis_size("grid")
    rows = 2 * orbitals
    width = extent // count
    lanes = proj_count * box
    size = wave.size * 4
    matrix = second_derivative(extent)
    kinds = species.reshape(1, atom_count)
    shares = lax.axis_size("orb")
    density_shape = shape((planes, extent // shares, extent))
    send = pl.pallas_call(
        functools.partial(pack_kernel, planes),
        out_shape=shape((count, rows, width * planes, extent)),
        grid=(planes,),
        in_specs=[pl.BlockSpec((2, orbitals, 1, extent, extent), lambda p: (0, 0, p, 0, 0))],
        out_specs=pl.BlockSpec((count, rows, width * planes, extent), lambda p: (0, 0, 0, 0)),
        compiler_params=params(),
        cost_estimate=cost(wave.size, 2 * size),
        name="pack",
    )(wave)
    held = lax.all_to_all(send, "grid", 0, 0, tiled=True)
    table = projectors.reshape(kind_count, box, proj_count, box, box)
    table = jnp.transpose(table, (0, 1, 3, 2, 4)).reshape(kind_count, box, box, lanes)
    table = jnp.pad(table, ((0, 0), (0, 1), (0, 0), (0, 0)))
    table = table.reshape(kind_count * (box + 1), box, lanes)
    coef = pl.pallas_call(
        project_kernel,
        out_shape=shape((rows, proj_count, atom_count)),
        in_specs=[VMEM] * 4 + [SMEM] * 2,
        out_specs=VMEM,
        scratch_shapes=[
            pltpu.VMEM((rows * planes, extent + box, extent), jnp.float32),
            pltpu.VMEM((rows, atom_count, lanes), jnp.float32),
            pltpu.SMEM((atom_count + 8,), jnp.int32),
        ],
        compiler_params=params(),
        cost_estimate=cost(40 * wave.size, 20 * size),
        name="project",
    )(wave, table, coupling, kinds, centres, species)
    reach = (box + planes - 2) // planes
    coef = coef + sum(
        passed_along(coef, "grid", step) for hop in range(reach) for step in (hop + 1, -hop - 1)
    )
    local, *terms = pl.pallas_call(
        local_kernel,
        out_shape=[shape((rows * planes, extent + box, extent))] + [density_shape] * shares,
        in_specs=[VMEM] * 3 + [SMEM],
        out_specs=[VMEM] * (shares + 1),
        compiler_params=params(),
        cost_estimate=cost(12 * extent * wave.size, 3 * size),
        name="local",
    )(wave, potential, matrix, occupations)
    density = terms[0]
    for k in range(1, shares):
        density = density + passed_along(terms[k], "orb", k)
    along = pl.pallas_call(
        along_x_kernel,
        out_shape=shape(held.shape),
        in_specs=[VMEM, VMEM, pl.BlockSpec(memory_space=pl.ANY)],
        out_specs=VMEM,
        scratch_shapes=[pltpu.VMEM((extent, extent), jnp.float32)],
        compiler_params=params(),
        cost_estimate=cost(6 * extent * wave.size, 2 * size),
        name="along_x",
    )(held, matrix, coef)
    back = lax.all_to_all(along, "grid", 0, 0, tiled=True)
    local = pl.pallas_call(
        spread_kernel,
        out_shape=shape(local.shape),
        in_specs=[VMEM] * 3 + [SMEM] * 2,
        out_specs=VMEM,
        scratch_shapes=[
            pltpu.VMEM((rows, atom_count, lanes), jnp.float32),
            pltpu.SMEM((atom_count + 8,), jnp.int32),
        ],
        compiler_params=params(),
        cost_estimate=cost(40 * wave.size, 20 * size),
        name="spread",
    )(local, table, coef, centres, species)
    update = pl.pallas_call(
        finish_kernel,
        out_shape=shape(wave.shape),
        in_specs=[VMEM, VMEM],
        out_specs=VMEM,
        compiler_params=params(),
        cost_estimate=cost(4 * wave.size, 3 * size),
        name="finish",
    )(local, back)
    return (update, density)


def solution(mesh):
    placed = (
        P(None, "orb", "grid", None, None),
        P("grid", None, None),
        P("orb"),
        P(),
        P(),
        P(),
        P(),
    )
    return jax.shard_map(
        per_device,
        mesh=mesh,
        in_specs=placed,
        out_specs=(P(None, "orb", "grid", None, None), P("grid", "orb", None)),
        check_vma=False,
    )
```
